32 devices in a mesh: row: 2 (over x), col: 4 (over z), gz: 4 (over y, core).
Axes of the slice: x: 2, y: 2, z: 4, core: 2. Of those that a mesh axis runs over, the one named last changes fastest.
Arguments:
- density_matrix: bfloat16 [8192, 8192], P('row', 'col'), may hold values from -24 to 24
- block_pattern: int32 [128, 128], P('row', 'col'), may hold values from 0 to 1, as said below
- tile_lists: int32 [32, 16], replicated, may hold values from 0 to 127, as said below
- basis_values: bfloat16 [2, 4, 4, 1024, 384], P('row', 'col', 'gz'), may hold values from -0.09375 to 0.09375
- core_density: float32 [4, 32, 96], P('row', 'col', 'gz'), may hold values from 0.5 to 4
- orbitals: float32 [8192, 128], P(('col', 'gz')), may hold values from -6 to 6
Outputs:
- hamiltonian: float32 [8192, 8192], P('row', ('col', 'gz'))
- applied: float32 [8192, 128], P(('row', 'col', 'gz'))
The draws below stay inside these ranges and needn't reach their ends.
Inputs may be any that keep to these rules, and one draw needn't show every extreme that they name: `block_pattern`: Symmetric, with ones on the diagonal. `tile_lists`: each row is increasing and holds exactly 4 block ids from every run of 32 ids that starts at a multiple of 32.
All inputs are finite; a program needn't handle non-finite values.
Results may differ from the reference program's by a relative error of at most 0.00048.
Values may be sent and summed in bfloat16 or wider, within the bound.
A program may use at most 256 MiB of HBM per device.

```python
import math
import jax
import jax.numpy as jnp
from jax import lax

NB = 8192
BS = 64
NORB = 128
TL = 16
TX = 2
TY = 8
TZ = 24
NBLK = 128
GROUP = 32
KC = 4
OV = 1024
CELLS = 384
NX = 4
NY = 32
NZ = 96
N_ROW = 2
N_COL = 4
N_GZ = 4
DEVICES = 32


def listed_blocks(key):
    key_list = jax.random.split(jax.random.fold_in(key, 17), DEVICES * N_COL)

    def choose(subkey):
        return jnp.sort(jax.random.permutation(subkey, GROUP)[:KC])
    chosen = jax.vmap(choose)(key_list).reshape(DEVICES, N_COL, KC).astype(jnp.int32)
    offsets = (jnp.arange(N_COL, dtype=jnp.int32) * GROUP)[None, :, None]
    return (chosen + offsets).reshape(DEVICES, TL).astype(jnp.int32)


def draw_tile_lists(key, part):
    return listed_blocks(key)


def draw_block_pattern(key, part):
    random_bits = jax.random.randint(jax.random.fold_in(key, 23), (NBLK, NBLK), 0, 2)
    row_ids = jnp.arange(NBLK, dtype=jnp.int32)[:, None]
    col_ids = jnp.arange(NBLK, dtype=jnp.int32)[None, :]
    mirrored = jnp.where(row_ids < col_ids, random_bits, random_bits.T)
    lists = listed_blocks(key)
    full_count = max(2, DEVICES // 64)
    full_tiles = jax.random.permutation(jax.random.fold_in(key, 29), DEVICES)[:full_count]
    full_lists = jnp.take(lists, full_tiles, axis=0)
    block_ids = jnp.arange(NBLK, dtype=jnp.int32)
    member = jnp.max((full_lists[:, :, None] == block_ids[None, None, :]).astype(jnp.int32), axis=1)
    covered = jnp.max(member[:, :, None] * member[:, None, :], axis=0)
    joined = jnp.maximum(mirrored, covered)
    return jnp.where(row_ids == col_ids, 1, joined).astype(jnp.int32)


def levels(rng, shape, cuts, low, largest):
    factor_of = 1.0
    for dim, shards_of in cuts:
        heights = jax.random.uniform(jax.random.fold_in(jax.random.fold_in(rng, 6), dim), (shards_of,), jnp.float32, low / len(cuts), largest / len(cuts))
        factor_of = factor_of * jnp.repeat(jnp.exp(heights), shape[dim] // shards_of).reshape((-1,) + (1,) * (len(shape) - 1 - dim))
    return factor_of


def scatter_about(own_key, dims, width, reach, cuts=(), held_as=jnp.bfloat16):
    factor_of = levels(own_key, dims, cuts, -0.22, 0.18) if cuts else 1.0
    array = jax.random.normal(own_key, dims, jnp.float32) * width * factor_of
    return jnp.minimum(jnp.maximum(array, -reach), reach).astype(held_as)


def setup_inputs(seed: int = 0) -> dict:
    seeds = jax.random.split(jax.random.key(seed), 7)
    density_matrix = scatter_about(seeds[0], (NB, NB), 4.0, 24.0, ((0, 2), (1, 4)))
    block_pattern = draw_block_pattern(jax.random.fold_in(seeds[6], 71), 0)
    tile_lists = draw_tile_lists(jax.random.fold_in(seeds[6], 71), 0)
    basis_values = scatter_about(seeds[3], (N_ROW, N_COL, N_GZ, OV, CELLS), 0.015625, 0.09375, ((0, 2), (1, 4), (2, 4)))
    core_density = jnp.clip(jnp.exp(math.log(4.0) - 2.0794415 * jax.random.uniform(seeds[4], (NX, NY, NZ), jnp.float32) ** levels(seeds[4], (NX, NY, NZ), ((0, 2), (1, 4), (2, 4)), -0.2, 0.2)), 0.5, 4.0)
    orbitals = scatter_about(seeds[5], (NB, NORB), 1.0, 6.0, ((0, 16),), jnp.float32)
    return {"density_matrix": density_matrix, "block_pattern": block_pattern, "tile_lists": tile_lists, "basis_values": basis_values, "core_density": core_density, "orbitals": orbitals}


pbe_kappa = 0.804
pbe_mu = 0.2195149727645171
exch_const = 0.75 * (3.0 / 3.141592653589793) ** (1.0 / 3.0)
grad_scale = 4.0 * (3.0 * 3.141592653589793 ** 2) ** (2.0 / 3.0)
density_floor = 0.2
spacing = 0.125

def energy(density, grad_square):
    scaled = grad_square / (grad_scale * density ** (8.0 / 3.0))
    enhance = 1.0 + pbe_kappa - pbe_kappa / (1.0 + pbe_mu * scaled / pbe_kappa)
    return -exch_const * density ** (4.0 / 3.0) * enhance

def total_energy(density, grad_square):
    return jnp.sum(energy(density, grad_square))

def centered(grid_values, direction):
    return (jnp.roll(grid_values, -1, direction) - jnp.roll(grid_values, 1, direction)) / (2.0 * spacing)

def potential(density):
    gradients = [centered(density, direction) for direction in range(3)]
    grad_square = gradients[0] * gradients[0] + gradients[1] * gradients[1] + gradients[2] * gradients[2]
    first, second = jax.grad(total_energy, argnums=(0, 1))(density, grad_square)
    divergence = jnp.zeros_like(density)
    for direction in range(3):
        divergence = divergence + centered(2.0 * second * gradients[direction], direction)
    return first - divergence

def reference(density_matrix, block_pattern, tile_lists, basis_values, core_density, orbitals):
    keep_mask = block_pattern.astype(jnp.bfloat16)
    masked = density_matrix.reshape(NBLK, BS, NBLK, BS) * keep_mask[:, None, :, None]
    tile_phi = basis_values.reshape(DEVICES, OV, CELLS)

    def tile_density(inputs):
        listed, phi_tile = inputs
        picked = jnp.take(masked, listed, axis=0)
        local_matrix = jnp.take(picked, listed, axis=2).reshape(OV, OV)
        product = jnp.dot(local_matrix, phi_tile, preferred_element_type=jnp.float32)
        return lax.optimization_barrier(jnp.sum(phi_tile.astype(jnp.float32) * product, axis=0))
    rho_tiles = lax.map(tile_density, (tile_lists, tile_phi))
    rho_grid = rho_tiles.reshape(N_ROW, N_COL, N_GZ, TX, TY, TZ).transpose(0, 3, 1, 4, 2, 5).reshape(NX, NY, NZ)
    density = jnp.maximum(rho_grid + core_density, density_floor)
    field = potential(density)
    field_tiles = field.reshape(N_ROW, TX, N_COL, TY, N_GZ, TZ).transpose(0, 2, 4, 1, 3, 5).reshape(DEVICES, CELLS)

    def add_tile(total, inputs):
        listed, phi_tile, tile_field = inputs
        weighted = (phi_tile.astype(jnp.float32) * tile_field[None, :]).astype(jnp.bfloat16)
        local_ham = lax.dot_general(weighted, phi_tile, (((1,), (1,)), ((), ())), preferred_element_type=jnp.float32)
        local_ham = local_ham.reshape(TL, BS, TL, BS).transpose(0, 2, 1, 3)
        total = total.at[listed[:, None], listed[None, :]].add(local_ham)
        return (total, None)
    start = jnp.zeros((NBLK, NBLK, BS, BS), jnp.float32)
    summed, unused = lax.scan(add_tile, start, (tile_lists, tile_phi, field_tiles))
    summed = summed * block_pattern.astype(jnp.float32)[:, :, None, None]
    hamiltonian = summed.transpose(0, 2, 1, 3).reshape(NB, NB)
    applied = jnp.dot(hamiltonian, orbitals, precision=lax.Precision.HIGHEST, preferred_element_type=jnp.float32)
    return (hamiltonian, applied)
```

```python
import jax
import jax.numpy as jnp
from jax import lax
from jax.experimental import pallas as pl
from jax.experimental.pallas import tpu as pltpu
from jax.sharding import PartitionSpec as P

pbe_kappa = 0.804
pbe_mu = 0.2195149727645171
exch_const = 0.75 * (3.0 / 3.141592653589793) ** (1.0 / 3.0)
grad_scale = 4.0 * (3.0 * 3.141592653589793**2) ** (2.0 / 3.0)
density_floor = 0.2
spacing = 0.125


def with_halo(cells, sides, width):
    for axis, dim in sides:
        count = lax.axis_size(axis)
        head = lax.slice_in_dim(cells, 0, width, axis=dim)
        tail = lax.slice_in_dim(cells, cells.shape[dim] - width, cells.shape[dim], axis=dim)
        cells = jnp.concatenate(
            [
                lax.ppermute(tail, axis, [(i, (i + 1) % count) for i in range(count)]),
                cells,
                lax.ppermute(head, axis, [((i + 1) % count, i) for i in range(count)]),
            ],
            axis=dim,
        )
    return cells


def energy(density, grad_square):
    scaled = grad_square / (grad_scale * density ** (8.0 / 3.0))
    enhance = 1.0 + pbe_kappa - pbe_kappa / (1.0 + pbe_mu * scaled / pbe_kappa)
    return -exch_const * density ** (4.0 / 3.0) * enhance


def total_energy(density, grad_square):
    return jnp.sum(energy(density, grad_square))


def centered(grid_values, direction):
    higher = [slice(1, -1), slice(1, -1), slice(1, -1)]
    lesser = [slice(1, -1), slice(1, -1), slice(1, -1)]
    higher[direction] = slice(2, None)
    lesser[direction] = slice(None, -2)
    return (grid_values[tuple(higher)] - grid_values[tuple(lesser)]) / (2.0 * spacing)


def potential_twice(density):
    padded = with_halo(density, (("row", 0), ("col", 1), ("gz", 2)), 1)
    gradients = [centered(padded, direction) for direction in range(3)]
    grad_square = (
        gradients[0] * gradients[0] + gradients[1] * gradients[1] + gradients[2] * gradients[2]
    )
    first, second = jax.grad(total_energy, argnums=(0, 1))(density, grad_square)
    fluxes = jnp.stack([2.0 * second * gradients[direction] for direction in range(3)])
    flux_ext = with_halo(fluxes, (("row", 1), ("col", 2), ("gz", 3)), 1)
    divergence = centered(flux_ext[0], 0) + centered(flux_ext[1], 1) + centered(flux_ext[2], 2)
    return first - divergence


def exchanged(density_matrix, block_pattern, tile_lists, basis_values, core_density, orbitals):
    row_count = lax.axis_size("row")
    column_count = lax.axis_size("col")
    depth_count = lax.axis_size("gz")
    row_index = lax.axis_index("row")
    column_index = lax.axis_index("col")
    depth_index = lax.axis_index("gz")
    row_blocks, column_blocks = block_pattern.shape
    block_size = density_matrix.shape[0] // row_blocks
    listed = tile_lists.shape[1]
    per_row = listed // row_count
    per_column = listed // column_count
    width = listed * block_size
    block_area = block_size * block_size
    slab_lists = tile_lists.reshape(row_count, column_count, depth_count, listed)
    slab_lists = lax.dynamic_index_in_dim(slab_lists, depth_index, axis=2, keepdims=False)
    mine_rows = (
        lax.dynamic_slice_in_dim(slab_lists, row_index * per_row, per_row, 2)
        - row_index * row_blocks
    )
    mine_cols = (
        lax.dynamic_slice_in_dim(slab_lists, column_index * per_column, per_column, 2)
        - column_index * column_blocks
    )
    block_ids = (mine_rows[:, :, :, None] * column_blocks + mine_cols[:, :, None, :]).reshape(-1)
    pattern_flat = block_pattern.reshape(-1)
    stored = density_matrix.reshape(row_blocks, block_size, column_blocks, block_size)
    stored = stored.transpose(0, 2, 1, 3).reshape(row_blocks * column_blocks, block_area)
    stored = stored * pattern_flat.astype(jnp.bfloat16)[:, None]
    outgoing = jnp.take(stored, block_ids, axis=0).reshape(
        row_count, column_count, per_row * per_column, block_area
    )
    flat_out = outgoing.reshape(row_count * column_count, per_row * per_column, block_area)
    incoming = lax.all_to_all(flat_out, ("row", "col"), split_axis=0, concat_axis=0, tiled=True)
    tile_matrix = incoming.reshape(
        row_count, column_count, per_row, per_column, block_size, block_size
    )
    tile_matrix = tile_matrix.transpose(0, 2, 4, 1, 3, 5).reshape(width, width)
    phi_tile = basis_values.reshape(width, -1)
    product = jnp.dot(tile_matrix, phi_tile, preferred_element_type=jnp.float32)
    rho_tile = jnp.sum(phi_tile * product, axis=0).reshape(core_density.shape)
    density = jnp.maximum(rho_tile + core_density, density_floor)
    field = potential_twice(density)
    weighted = (phi_tile * field.reshape(1, -1)).astype(jnp.bfloat16)
    local_ham = lax.dot_general(
        weighted, phi_tile, (((1,), (1,)), ((), ())), preferred_element_type=jnp.float32
    )
    returning = local_ham.reshape(
        row_count, per_row, block_size, column_count, per_column, block_size
    )
    returning = returning.transpose(0, 3, 1, 4, 2, 5).reshape(
        row_count, column_count, per_row * per_column, block_area
    )
    flat_back = returning.reshape(row_count * column_count, per_row * per_column, block_area)
    arrived = lax.all_to_all(flat_back, ("row", "col"), split_axis=0, concat_axis=0, tiled=True)
    owned = jnp.zeros((row_blocks * column_blocks, block_area), jnp.float32)
    owned = owned.at[block_ids].add(arrived.reshape(-1, block_area))
    owned = owned * pattern_flat.astype(jnp.float32)[:, None]
    dense = owned.reshape(row_blocks, column_blocks, block_size, block_size)
    dense = dense.transpose(0, 2, 1, 3).reshape(row_blocks * block_size, column_blocks * block_size)
    share = lax.psum_scatter(dense, "gz", scatter_dimension=1, tiled=True)
    terms = jnp.dot(
        share, orbitals, precision=lax.Precision.HIGHEST, preferred_element_type=jnp.float32
    )
    applied = lax.psum_scatter(terms, ("col", "gz"), scatter_dimension=0, tiled=True)
    return (share, applied)


vmem_bytes = 56 * 1024 * 1024
gathered_limit = 48 * 1024 * 1024


def density_kernel(per_row, per_column, size, rows_ref, cols_ref, keep_ref, place_ref, *refs):
    strips = refs[:per_row]
    phi_rows, phi_cols, out, picked, padded = refs[per_row:]
    tile = pl.program_id(0)
    pair_width = 2 * size
    for n in range(per_column):
        column = cols_ref[tile, n]
        start = pl.multiple_of((column // 2) * pair_width, pair_width)
        odd = column % 2
        values = phi_cols[0, n * size : (n + 1) * size, :]
        for half in range(2):
            padded[n * pair_width + half * size : n * pair_width + (half + 1) * size, :] = (
                jnp.where(odd == half, values, jnp.zeros_like(values))
            )
        for m in range(per_row):
            block = strips[m][:, pl.ds(start, pair_width)]
            kept = keep_ref[tile, m * per_column + n] != 0
            picked[m * size : (m + 1) * size, n * pair_width : (n + 1) * pair_width] = jnp.where(
                kept, block, jnp.zeros_like(block)
            )
    product = jnp.dot(picked[...], padded[...], preferred_element_type=jnp.float32)
    rho = jnp.sum(phi_rows[0].astype(jnp.float32) * product, axis=0, keepdims=True)
    out[0] = rho


def partial_density(density_matrix, slab_phi, rows, cols, keep, place, size):
    tiles, width, cells = slab_phi.shape
    per_row, per_column = rows.shape[1], cols.shape[1]
    columns = density_matrix.shape[1]

    def strip_spec(m):
        return pl.BlockSpec((size, columns), lambda t, rows, cols, keep, place: (rows[t, m], 0))

    grid_spec = pltpu.PrefetchScalarGridSpec(
        num_scalar_prefetch=4,
        grid=(tiles,),
        in_specs=[strip_spec(m) for m in range(per_row)]
        + [
            pl.BlockSpec(
                (1, per_row * size, cells), lambda t, rows, cols, keep, place: (t, place[0], 0)
            ),
            pl.BlockSpec(
                (1, per_column * size, cells), lambda t, rows, cols, keep, place: (t, place[1], 0)
            ),
        ],
        out_specs=pl.BlockSpec((1, 1, cells), lambda t, rows, cols, keep, place: (t, 0, 0)),
        scratch_shapes=[
            pltpu.VMEM((per_row * size, 2 * per_column * size), jnp.bfloat16),
            pltpu.VMEM((2 * per_column * size, cells), jnp.bfloat16),
        ],
    )

    def body(*refs):
        density_kernel(per_row, per_column, size, *refs)

    return pl.pallas_call(
        body,
        grid_spec=grid_spec,
        out_shape=jax.ShapeDtypeStruct((tiles, 1, cells), jnp.float32),
        compiler_params=pltpu.CompilerParams(vmem_limit_bytes=vmem_bytes),
        cost_estimate=pl.CostEstimate(
            flops=4 * tiles * per_row * per_column * size * size * cells,
            bytes_accessed=tiles * per_row * size * columns * 2,
            transcendentals=0,
        ),
        name="partial_density",
    )(rows, cols, keep, place, *([density_matrix] * per_row), slab_phi, slab_phi)


def hamiltonian_kernel(
    per_row, size, owned, rows_ref, from_ref, place_ref, phi_rows, phi_cols, field, keep, orbitals,
    out, terms, total, weighted, padded,
):
    tile = pl.program_id(0)
    pair_width = 2 * size

    @pl.when(tile == 0)
    def _():
        total[...] = jnp.zeros_like(total)

    weighted[...] = (phi_rows[0].astype(jnp.float32) * field[0]).astype(jnp.bfloat16)
    for pair in range(owned // 2):
        left = from_ref[tile, 2 * pair]
        right = from_ref[tile, 2 * pair + 1]

        @pl.when(jnp.maximum(left, right) >= 0)
        def _():
            for half, source in enumerate((left, right)):
                start = pl.multiple_of(jnp.maximum(source, 0) * size, size)
                values = phi_cols[0, pl.ds(start, size), :]
                padded[half * size : (half + 1) * size, :] = jnp.where(
                    source >= 0, values, jnp.zeros_like(values)
                )
            product = lax.dot_general(
                weighted[...],
                padded[...],
                (((1,), (1,)), ((), ())),
                preferred_element_type=jnp.float32,
            )
            span = slice(pair * pair_width, (pair + 1) * pair_width)
            for m in range(per_row):
                start = pl.multiple_of(rows_ref[tile, m] * size, size)
                total[pl.ds(start, size), span] += product[m * size : (m + 1) * size]

    @pl.when(tile == pl.num_programs(0) - 1)
    def _():
        step = 4 * size

        @pl.loop(0, total.shape[0] // step)
        def _(chunk):
            for part in range(4):
                span = pl.ds(pl.multiple_of(chunk * step + part * size, size), size)
                out[span, :] = total[span, :] * keep[pl.ds(chunk * 4 + part, 1), :]
            span = pl.ds(pl.multiple_of(chunk * step, step), step)
            terms[span, :] = jnp.dot(
                out[span, :],
                orbitals[...],
                precision=lax.Precision.HIGHEST,
                preferred_element_type=jnp.float32,
            )


def owned_hamiltonian(phi, field, rows, sources, place, keep, orbitals, size, per_column):
    tiles, width, cells = phi.shape
    per_row = rows.shape[1]
    owned = sources.shape[1]
    high = keep.shape[0] * size
    wide = owned * size
    norb = orbitals.shape[1]
    grid_spec = pltpu.PrefetchScalarGridSpec(
        num_scalar_prefetch=3,
        grid=(tiles,),
        in_specs=[
            pl.BlockSpec((1, per_row * size, cells), lambda t, rows, sources, place: (t, place[0], 0)),
            pl.BlockSpec(
                (1, per_column * size, cells), lambda t, rows, sources, place: (t, place[1], 0)
            ),
            pl.BlockSpec((1, 1, cells), lambda t, rows, sources, place: (t, 0, 0)),
            pl.BlockSpec(keep.shape, lambda t, rows, sources, place: (0, 0)),
            pl.BlockSpec(orbitals.shape, lambda t, rows, sources, place: (0, 0)),
        ],
        out_specs=[
            pl.BlockSpec((high, wide), lambda t, rows, sources, place: (0, 0)),
            pl.BlockSpec((high, norb), lambda t, rows, sources, place: (0, 0)),
        ],
        scratch_shapes=[
            pltpu.VMEM((high, wide), jnp.float32),
            pltpu.VMEM((per_row * size, cells), jnp.bfloat16),
            pltpu.VMEM((2 * size, cells), jnp.bfloat16),
        ],
    )

    def body(*refs):
        hamiltonian_kernel(per_row, size, owned, *refs)

    return pl.pallas_call(
        body,
        grid_spec=grid_spec,
        out_shape=[
            jax.ShapeDtypeStruct((high, wide), jnp.float32),
            jax.ShapeDtypeStruct((high, norb), jnp.float32),
        ],
        compiler_params=pltpu.CompilerParams(vmem_limit_bytes=vmem_bytes),
        name="owned_hamiltonian",
    )(rows, sources, place, phi, phi, field, keep, orbitals)


def whole_potential(density):
    def difference(values, direction):
        return (jnp.roll(values, -1, direction) - jnp.roll(values, 1, direction)) / (2.0 * spacing)

    gradients = [difference(density, direction) for direction in range(3)]
    grad_square = (
        gradients[0] * gradients[0] + gradients[1] * gradients[1] + gradients[2] * gradients[2]
    )
    first, second = jax.grad(total_energy, argnums=(0, 1))(density, grad_square)
    divergence = sum(
        difference(2.0 * second * gradients[direction], direction) for direction in range(3)
    )
    return first - divergence


def gathered(density_matrix, block_pattern, tile_lists, basis_values, core_density, orbitals):
    row_count = lax.axis_size("row")
    column_count = lax.axis_size("col")
    depth_count = lax.axis_size("gz")
    row_index = lax.axis_index("row")
    column_index = lax.axis_index("col")
    depth_index = lax.axis_index("gz")
    row_blocks, column_blocks = block_pattern.shape
    size = density_matrix.shape[0] // row_blocks
    tiles, listed = tile_lists.shape
    per_row = listed // row_count
    per_column = listed // column_count
    owned = column_blocks // depth_count
    cells = core_density.size
    phi_tile = basis_values.reshape(listed * size, cells)

    lists = tile_lists.reshape(row_count, column_count, depth_count, listed).transpose(2, 0, 1, 3)
    lists = lists.reshape(tiles, listed)
    rows = lax.dynamic_slice_in_dim(lists, row_index * per_row, per_row, 1) - row_index * row_blocks
    cols = (
        lax.dynamic_slice_in_dim(lists, column_index * per_column, per_column, 1)
        - column_index * column_blocks
    )
    slab = row_count * column_count
    slab_rows = lax.dynamic_slice_in_dim(rows, depth_index * slab, slab, 0)
    slab_cols = lax.dynamic_slice_in_dim(cols, depth_index * slab, slab, 0)
    slab_keep = block_pattern[slab_rows[:, :, None], slab_cols[:, None, :]]
    slab_keep = slab_keep.reshape(slab, per_row * per_column)
    place = jnp.stack([row_index, column_index]).astype(jnp.int32)
    own_ids = depth_index * owned + jnp.arange(owned, dtype=jnp.int32)
    matches = cols[:, None, :] == own_ids[None, :, None]
    numbers = jnp.arange(per_column, dtype=jnp.int32)[None, None, :]
    sources = jnp.max(jnp.where(matches, numbers, -1), axis=2).astype(jnp.int32)
    own_pattern = lax.dynamic_slice_in_dim(block_pattern, depth_index * owned, owned, 1)
    keep = jnp.repeat(own_pattern.astype(jnp.float32), size, axis=1)

    slab_phi = lax.all_gather(phi_tile, ("row", "col"), axis=0, tiled=False)
    slab_phi = slab_phi.reshape(slab, listed * size, cells)
    phi = lax.all_gather(slab_phi, "gz", axis=0, tiled=True)

    partial = partial_density(
        density_matrix, slab_phi, slab_rows, slab_cols, slab_keep, place, size
    )
    partial = partial.reshape(slab, cells)
    own_tile = (row_index * column_count + column_index) == jnp.arange(slab)[:, None]
    partial = partial + jnp.where(own_tile, core_density.reshape(1, cells), 0.0)
    parts = lax.all_gather(partial, ("row", "col", "gz"), axis=0, tiled=False)
    parts = parts.reshape(slab, depth_count, slab, cells).sum(axis=0)
    tile_shape = core_density.shape
    grid = parts.reshape((depth_count, row_count, column_count) + tile_shape)
    grid = grid.transpose(1, 3, 2, 4, 0, 5).reshape(
        row_count * tile_shape[0], column_count * tile_shape[1], depth_count * tile_shape[2]
    )
    field = whole_potential(jnp.maximum(grid, density_floor))
    field = field.reshape(
        row_count, tile_shape[0], column_count, tile_shape[1], depth_count, tile_shape[2]
    )
    field = field.transpose(4, 0, 2, 1, 3, 5).reshape(tiles, 1, cells)
    hamiltonian, terms = owned_hamiltonian(
        phi, field, rows, sources, place, keep, orbitals, size, per_column
    )
    applied = lax.psum_scatter(terms, ("col", "gz"), scatter_dimension=0, tiled=True)
    return hamiltonian, applied


def shards(density_matrix, block_pattern, tile_lists, basis_values, core_density, orbitals):
    arguments = (
        density_matrix, block_pattern, tile_lists, basis_values, core_density, orbitals,
    )
    fits = tile_lists.shape[0] * basis_values.size * 2 <= gathered_limit
    return gathered(*arguments) if fits else exchanged(*arguments)


def solution(mesh):
    placed = (
        P("row", "col"),
        P("row", "col"),
        P(),
        P("row", "col", "gz", None, None),
        P("row", "col", "gz"),
        P(("col", "gz"), None),
    )
    return jax.shard_map(
        shards,
        mesh=mesh,
        in_specs=placed,
        out_specs=(P("row", ("col", "gz")), P(("row", "col", "gz"), None)),
        check_vma=False,
    )
```

```python
import jax
import jax.numpy as jnp
from jax import lax
from jax.experimental import pallas as pl
from jax.experimental.pallas import tpu as pltpu
from jax.sharding import PartitionSpec as P

pbe_kappa = 0.804
pbe_mu = 0.2195149727645171
exch_const = 0.75 * (3.0 / 3.141592653589793) ** (1.0 / 3.0)
grad_scale = 4.0 * (3.0 * 3.141592653589793**2) ** (2.0 / 3.0)
density_floor = 0.2
spacing = 0.125


def with_halo(cells, sides, width):
    for axis, dim in sides:
        count = lax.axis_size(axis)
        head = lax.slice_in_dim(cells, 0, width, axis=dim)
        tail = lax.slice_in_dim(cells, cells.shape[dim] - width, cells.shape[dim], axis=dim)
        cells = jnp.concatenate(
            [
                lax.ppermute(tail, axis, [(i, (i + 1) % count) for i in range(count)]),
                cells,
                lax.ppermute(head, axis, [((i + 1) % count, i) for i in range(count)]),
            ],
            axis=dim,
        )
    return cells


def energy(density, grad_square):
    scaled = grad_square / (grad_scale * density ** (8.0 / 3.0))
    enhance = 1.0 + pbe_kappa - pbe_kappa / (1.0 + pbe_mu * scaled / pbe_kappa)
    return -exch_const * density ** (4.0 / 3.0) * enhance


def total_energy(density, grad_square):
    return jnp.sum(energy(density, grad_square))


def centered(grid_values, direction):
    higher = [slice(1, -1), slice(1, -1), slice(1, -1)]
    lesser = [slice(1, -1), slice(1, -1), slice(1, -1)]
    higher[direction] = slice(2, None)
    lesser[direction] = slice(None, -2)
    return (grid_values[tuple(higher)] - grid_values[tuple(lesser)]) / (2.0 * spacing)


def potential_twice(density):
    padded = with_halo(density, (("row", 0), ("col", 1), ("gz", 2)), 1)
    gradients = [centered(padded, direction) for direction in range(3)]
    grad_square = (
        gradients[0] * gradients[0] + gradients[1] * gradients[1] + gradients[2] * gradients[2]
    )
    first, second = jax.grad(total_energy, argnums=(0, 1))(density, grad_square)
    fluxes = jnp.stack([2.0 * second * gradients[direction] for direction in range(3)])
    flux_ext = with_halo(fluxes, (("row", 1), ("col", 2), ("gz", 3)), 1)
    divergence = centered(flux_ext[0], 0) + centered(flux_ext[1], 1) + centered(flux_ext[2], 2)
    return first - divergence


def exchanged(density_matrix, block_pattern, tile_lists, basis_values, core_density, orbitals):
    row_count = lax.axis_size("row")
    column_count = lax.axis_size("col")
    depth_count = lax.axis_size("gz")
    row_index = lax.axis_index("row")
    column_index = lax.axis_index("col")
    depth_index = lax.axis_index("gz")
    row_blocks, column_blocks = block_pattern.shape
    block_size = density_matrix.shape[0] // row_blocks
    listed = tile_lists.shape[1]
    per_row = listed // row_count
    per_column = listed // column_count
    width = listed * block_size
    block_area = block_size * block_size
    slab_lists = tile_lists.reshape(row_count, column_count, depth_count, listed)
    slab_lists = lax.dynamic_index_in_dim(slab_lists, depth_index, axis=2, keepdims=False)
    mine_rows = (
        lax.dynamic_slice_in_dim(slab_lists, row_index * per_row, per_row, 2)
        - row_index * row_blocks
    )
    mine_cols = (
        lax.dynamic_slice_in_dim(slab_lists, column_index * per_column, per_column, 2)
        - column_index * column_blocks
    )
    block_ids = (mine_rows[:, :, :, None] * column_blocks + mine_cols[:, :, None, :]).reshape(-1)
    pattern_flat = block_pattern.reshape(-1)
    stored = density_matrix.reshape(row_blocks, block_size, column_blocks, block_size)
    stored = stored.transpose(0, 2, 1, 3).reshape(row_blocks * column_blocks, block_area)
    stored = stored * pattern_flat.astype(jnp.bfloat16)[:, None]
    outgoing = jnp.take(stored, block_ids, axis=0).reshape(
        row_count, column_count, per_row * per_column, block_area
    )
    flat_out = outgoing.reshape(row_count * column_count, per_row * per_column, block_area)
    incoming = lax.all_to_all(flat_out, ("row", "col"), split_axis=0, concat_axis=0, tiled=True)
    tile_matrix = incoming.reshape(
        row_count, column_count, per_row, per_column, block_size, block_size
    )
    tile_matrix = tile_matrix.transpose(0, 2, 4, 1, 3, 5).reshape(width, width)
    phi_tile = basis_values.reshape(width, -1)
    product = jnp.dot(tile_matrix, phi_tile, preferred_element_type=jnp.float32)
    rho_tile = jnp.sum(phi_tile * product, axis=0).reshape(core_density.shape)
    density = jnp.maximum(rho_tile + core_density, density_floor)
    field = potential_twice(density)
    weighted = (phi_tile * field.reshape(1, -1)).astype(jnp.bfloat16)
    local_ham = lax.dot_general(
        weighted, phi_tile, (((1,), (1,)), ((), ())), preferred_element_type=jnp.float32
    )
    returning = local_ham.reshape(
        row_count, per_row, block_size, column_count, per_column, block_size
    )
    returning = returning.transpose(0, 3, 1, 4, 2, 5).reshape(
        row_count, column_count, per_row * per_column, block_area
    )
    flat_back = returning.reshape(row_count * column_count, per_row * per_column, block_area)
    arrived = lax.all_to_all(flat_back, ("row", "col"), split_axis=0, concat_axis=0, tiled=True)
    owned = jnp.zeros((row_blocks * column_blocks, block_area), jnp.float32)
    owned = owned.at[block_ids].add(arrived.reshape(-1, block_area))
    owned = owned * pattern_flat.astype(jnp.float32)[:, None]
    dense = owned.reshape(row_blocks, column_blocks, block_size, block_size)
    dense = dense.transpose(0, 2, 1, 3).reshape(row_blocks * block_size, column_blocks * block_size)
    share = lax.psum_scatter(dense, "gz", scatter_dimension=1, tiled=True)
    terms = jnp.dot(
        share, orbitals, precision=lax.Precision.HIGHEST, preferred_element_type=jnp.float32
    )
    applied = lax.psum_scatter(terms, ("col", "gz"), scatter_dimension=0, tiled=True)
    return (share, applied)


vmem_bytes = 56 * 1024 * 1024
gathered_limit = 48 * 1024 * 1024


MESH = pl.DeviceIdType.MESH


def meet(peers):
    barrier = pltpu.get_barrier_semaphore()
    for peer in peers:
        pl.semaphore_signal(barrier, inc=1, device_id=peer, device_id_type=MESH)
    pl.semaphore_wait(barrier, len(peers))


def basis_kernel(row_count, column_count, phi, rows_out, cols_out, own_sem, send, got, got_cols):
    i, j, k = lax.axis_index("row"), lax.axis_index("col"), lax.axis_index("gz")
    across = 1 - i
    beside = lax.rem(k + 2, 4)
    twin = k + 1 - 2 * lax.rem(k, 2)
    half = column_count // row_count
    share = phi.shape[1] // half
    provider = (j // half) == i
    offset = pl.multiple_of(lax.rem(j, half) * share, share)
    others = [lax.rem(j + step, column_count) for step in range(1, column_count)]
    x_peer, y_peer, c_peer = (across, j, k), (i, j, beside), (i, j, twin)
    z_peers = [(i, other, k) for other in others]
    meet([x_peer, y_peer, c_peer] + z_peers)
    started, started_cols, started_twin = [], [], []

    def push(source, target, arrival, peer, log):
        number = len(started) + len(started_cols) + len(started_twin)
        copy = pltpu.make_async_remote_copy(
            src_ref=source, dst_ref=target, send_sem=send.at[number], recv_sem=arrival,
            device_id=peer, device_id_type=MESH,
        )
        log.append(copy)
        return copy

    def arrived(out, sems, where):
        pltpu.make_async_remote_copy(
            src_ref=out.at[where], dst_ref=out.at[where], send_sem=send.at[0],
            recv_sem=sems.at[where], device_id=x_peer, device_id_type=MESH,
        ).wait_recv()

    own = (k, i, j)
    local = pltpu.make_async_copy(phi.at[i], rows_out.at[own], own_sem)
    local.start()
    push(phi.at[across], rows_out.at[own], got.at[own], x_peer, started).start()

    queue = []

    def spread(source, where, along_z, along_y):
        if along_z:
            for peer in z_peers:
                push(source, rows_out.at[where], got.at[where], peer, started).start()
        if along_y:
            push(source, rows_out.at[where], got.at[where], y_peer, started).start()
        column = push(
            source.at[pl.ds(offset, share)], cols_out.at[where], got_cols.at[where], x_peer,
            started_cols,
        )
        pl.when(provider)(column.start)
        push(source, rows_out.at[where], got.at[where], c_peer, started).start()
        queue.append(where)
        if len(queue) > 3:
            relay(queue.pop(0))

    def relay(where):
        copy = push(
            cols_out.at[where], cols_out.at[where], got_cols.at[where], c_peer, started_twin
        )

        @pl.when(jnp.logical_not(provider))
        def _():
            arrived(cols_out, got_cols, where)
            copy.start()

    spread(phi.at[i], own, True, True)
    where = (k, across, j)
    arrived(rows_out, got, where)
    spread(rows_out.at[where], where, True, True)
    slab = [(side, other) for side in (i, across) for other in others]
    for side, other in slab:
        where = (k, side, other)
        arrived(rows_out, got, where)
        spread(rows_out.at[where], where, False, True)
    for side, other in [(i, j), (across, j)] + slab:
        where = (beside, side, other)
        arrived(rows_out, got, where)
        spread(rows_out.at[where], where, False, False)
    while queue:
        relay(queue.pop(0))
    for depth in (twin, lax.rem(twin + 2, 4)):
        for side, other in [(i, j), (across, j)] + slab:
            arrived(rows_out, got, (depth, side, other))

    @pl.when(jnp.logical_not(provider))
    def _():
        for depth in (twin, lax.rem(twin + 2, 4)):
            for side, other in [(i, j), (across, j)] + slab:
                arrived(cols_out, got_cols, (depth, side, other))
        for copy in started_twin:
            copy.wait_send()

    @pl.when(provider)
    def _():
        for copy in started_cols:
            copy.wait_send()

    for copy in started:
        copy.wait_send()
    local.wait()


def gather_basis(phi_tile, row_count, column_count, depth_count):
    width, cells = phi_tile.shape
    halves = phi_tile.reshape(row_count, width // row_count, cells)
    grid = (depth_count, row_count, column_count)
    count = row_count * column_count
    messages = 1 + row_count * (column_count - 1) + count + 3 * 2 * count

    def body(*refs):
        basis_kernel(row_count, column_count, *refs)

    rows_phi, cols_phi = pl.pallas_call(
        body,
        in_specs=[pl.BlockSpec(memory_space=pltpu.HBM)],
        out_specs=[pl.BlockSpec(memory_space=pltpu.HBM)] * 2,
        out_shape=[
            jax.ShapeDtypeStruct(grid + (width // row_count, cells), phi_tile.dtype),
            jax.ShapeDtypeStruct(grid + (width // column_count, cells), phi_tile.dtype),
        ],
        scratch_shapes=[
            pltpu.SemaphoreType.DMA,
            pltpu.SemaphoreType.DMA((messages,)),
            pltpu.SemaphoreType.DMA(grid),
            pltpu.SemaphoreType.DMA(grid),
        ],
        compiler_params=pltpu.CompilerParams(collective_id=0, has_side_effects=True),
        name="gather_basis",
    )(halves)
    tiles = depth_count * count
    return (
        rows_phi.reshape(tiles, width // row_count, cells),
        cols_phi.reshape(tiles, width // column_count, cells),
    )


def sum_kernel(row_count, column_count, depth_count, partial, out, slots, slabs, send, got, got_slab):
    i, j, k = lax.axis_index("row"), lax.axis_index("col"), lax.axis_index("gz")
    count = row_count * column_count
    me = i * column_count + j
    peers = [lax.rem(me + step, count) for step in range(1, count)]
    depths = [lax.rem(k + step, depth_count) for step in range(1, depth_count)]
    ids = [(peer // column_count, lax.rem(peer, column_count), k) for peer in peers]
    depth_ids = [(i, j, depth) for depth in depths]
    meet(ids + depth_ids)
    copies = []
    for number, peer in enumerate(ids):
        copy = pltpu.make_async_remote_copy(
            src_ref=partial, dst_ref=slots.at[me], send_sem=send.at[number],
            recv_sem=got.at[me], device_id=peer, device_id_type=MESH,
        )
        copy.start()
        copies.append(copy)
    slots[me] = partial[...]
    for peer in peers:
        pltpu.make_async_remote_copy(
            src_ref=partial, dst_ref=slots.at[peer], send_sem=send.at[0],
            recv_sem=got.at[peer], device_id=ids[0], device_id_type=MESH,
        ).wait_recv()
    summed = slots[0]
    for number in range(1, count):
        summed = summed + slots[number]
    slabs[k] = summed
    for number, peer in enumerate(depth_ids):
        copy = pltpu.make_async_remote_copy(
            src_ref=slabs.at[k], dst_ref=slabs.at[k], send_sem=send.at[count - 1 + number],
            recv_sem=got_slab.at[k], device_id=peer, device_id_type=MESH,
        )
        copy.start()
        copies.append(copy)
    for depth in depths:
        pltpu.make_async_remote_copy(
            src_ref=partial, dst_ref=slabs.at[depth], send_sem=send.at[0],
            recv_sem=got_slab.at[depth], device_id=ids[0], device_id_type=MESH,
        ).wait_recv()
    out[...] = slabs[...]
    for copy in copies:
        copy.wait_send()


def sum_density(partial, row_count, column_count, depth_count):
    count = row_count * column_count

    def body(*refs):
        sum_kernel(row_count, column_count, depth_count, *refs)

    return pl.pallas_call(
        body,
        in_specs=[pl.BlockSpec(memory_space=pltpu.VMEM)],
        out_specs=pl.BlockSpec(memory_space=pltpu.VMEM),
        out_shape=jax.ShapeDtypeStruct((depth_count,) + partial.shape, partial.dtype),
        scratch_shapes=[
            pltpu.VMEM((count,) + partial.shape, partial.dtype),
            pltpu.VMEM((depth_count,) + partial.shape, partial.dtype),
            pltpu.SemaphoreType.DMA((count + depth_count,)),
            pltpu.SemaphoreType.DMA((count,)),
            pltpu.SemaphoreType.DMA((depth_count,)),
        ],
        compiler_params=pltpu.CompilerParams(collective_id=1, has_side_effects=True),
        name="sum_density",
    )(partial)


def applied_kernel(column_count, terms, out, c_got, y_send, y_got, z_send, z_got, send, got):
    i, j, k = lax.axis_index("row"), lax.axis_index("col"), lax.axis_index("gz")
    y, c = k // 2, lax.rem(k, 2)
    y_peer, c_peer = (i, j, lax.rem(k + 2, 4)), (i, j, k + 1 - 2 * c)
    others = [lax.rem(j + step, column_count) for step in range(1, column_count)]
    z_peers = [(i, other, k) for other in others]
    meet([y_peer, c_peer] + z_peers)

    def push(number, source, target, peer):
        copy = pltpu.make_async_remote_copy(
            src_ref=source, dst_ref=target, send_sem=send.at[number], recv_sem=got.at[number],
            device_id=peer, device_id_type=MESH,
        )
        copy.start()
        return copy

    first = push(0, terms.at[1 - y, 1 - c], c_got.at[0], c_peer)
    second = push(1, terms.at[y, 1 - c], c_got.at[1], c_peer)
    first.wait_recv()
    y_send[...] = terms[1 - y, c] + c_got[0]
    third = push(2, y_send, y_got, y_peer)
    second.wait_recv()
    z_send[...] = terms[y, c] + c_got[1]
    third.wait_recv()
    z_send[...] = z_send[...] + y_got[...]
    last = []
    for number, (other, peer) in enumerate(zip(others, z_peers)):
        last.append(push(3 + number, z_send.at[other], z_got.at[number], peer))
    total = z_send[j]
    for number, copy in enumerate(last):
        copy.wait_recv()
        total = total + z_got[number]
    out[...] = total
    for copy in [first, second, third] + last:
        copy.wait_send()


def sum_applied(terms, column_count):
    high, norb = terms.shape
    rows = high // (4 * column_count)
    parts = terms.reshape(column_count, 2, 2, rows, norb).transpose(1, 2, 0, 3, 4)
    part = (column_count, rows, norb)

    def body(*refs):
        applied_kernel(column_count, *refs)

    return pl.pallas_call(
        body,
        in_specs=[pl.BlockSpec(memory_space=pltpu.VMEM)],
        out_specs=pl.BlockSpec(memory_space=pltpu.VMEM),
        out_shape=jax.ShapeDtypeStruct((rows, norb), terms.dtype),
        scratch_shapes=[
            pltpu.VMEM((2,) + part, terms.dtype),
            pltpu.VMEM(part, terms.dtype),
            pltpu.VMEM(part, terms.dtype),
            pltpu.VMEM(part, terms.dtype),
            pltpu.VMEM((column_count - 1, rows, norb), terms.dtype),
            pltpu.SemaphoreType.DMA((2 + column_count,)),
            pltpu.SemaphoreType.DMA((2 + column_count,)),
        ],
        compiler_params=pltpu.CompilerParams(
            collective_id=2, has_side_effects=True, vmem_limit_bytes=vmem_bytes // 2
        ),
        name="sum_applied",
    )(parts)


def density_kernel(per_row, per_column, size, rows_ref, cols_ref, keep_ref, place_ref, *refs):
    strips = refs[:per_row]
    phi_rows, phi_near, phi_far, out, picked, padded = refs[per_row:]
    tile = pl.program_id(0)
    pair_width = 2 * size
    for n in range(per_column):
        column = cols_ref[tile, n]
        start = pl.multiple_of((column // 2) * pair_width, pair_width)
        odd = column % 2
        span = slice(n * size, (n + 1) * size)
        values = jnp.where(place_ref[1] == 1, phi_near[0, span, :], phi_far[0, span, :])
        for half in range(2):
            padded[n * pair_width + half * size : n * pair_width + (half + 1) * size, :] = (
                jnp.where(odd == half, values, jnp.zeros_like(values))
            )
        for m in range(per_row):
            block = strips[m][:, pl.ds(start, pair_width)]
            kept = keep_ref[tile, m * per_column + n] != 0
            picked[m * size : (m + 1) * size, n * pair_width : (n + 1) * pair_width] = jnp.where(
                kept, block, jnp.zeros_like(block)
            )
    product = jnp.dot(picked[...], padded[...], preferred_element_type=jnp.float32)
    rho = jnp.sum(phi_rows[0].astype(jnp.float32) * product, axis=0, keepdims=True)
    out[0] = rho


def partial_density(density_matrix, rows_phi, cols_phi, rows, cols, keep, place, size):
    tiles, cells = rows.shape[0], rows_phi.shape[2]
    per_row, per_column = rows.shape[1], cols.shape[1]
    columns = density_matrix.shape[1]

    def strip_spec(m):
        return pl.BlockSpec((size, columns), lambda t, rows, cols, keep, place: (rows[t, m], 0))

    grid_spec = pltpu.PrefetchScalarGridSpec(
        num_scalar_prefetch=4,
        grid=(tiles,),
        in_specs=[strip_spec(m) for m in range(per_row)]
        + [
            pl.BlockSpec(
                (1, per_row * size, cells),
                lambda t, rows, cols, keep, place: (place[2] + t, 0, 0),
            ),
            pl.BlockSpec(
                (1, per_column * size, cells),
                lambda t, rows, cols, keep, place: ((place[2] + t) * place[1], place[0], 0),
            ),
            pl.BlockSpec(
                (1, per_column * size, cells),
                lambda t, rows, cols, keep, place: ((place[2] + t) * (1 - place[1]), 0, 0),
            ),
        ],
        out_specs=pl.BlockSpec((1, 1, cells), lambda t, rows, cols, keep, place: (t, 0, 0)),
        scratch_shapes=[
            pltpu.VMEM((per_row * size, 2 * per_column * size), jnp.bfloat16),
            pltpu.VMEM((2 * per_column * size, cells), jnp.bfloat16),
        ],
    )

    def body(*refs):
        density_kernel(per_row, per_column, size, *refs)

    return pl.pallas_call(
        body,
        grid_spec=grid_spec,
        out_shape=jax.ShapeDtypeStruct((tiles, 1, cells), jnp.float32),
        compiler_params=pltpu.CompilerParams(vmem_limit_bytes=vmem_bytes),
        cost_estimate=pl.CostEstimate(
            flops=4 * tiles * per_row * per_column * size * size * cells,
            bytes_accessed=tiles * per_row * size * columns * 2,
            transcendentals=0,
        ),
        name="partial_density",
    )(rows, cols, keep, place, *([density_matrix] * per_row), rows_phi, rows_phi, cols_phi)


def hamiltonian_kernel(
    per_row, size, owned, rows_ref, from_ref, place_ref, phi_rows, phi_near, phi_far, field, keep, orbitals,
    out, terms, total, weighted, padded,
):
    tile = pl.program_id(0)
    pair_width = 2 * size

    @pl.when(tile == 0)
    def _():
        total[...] = jnp.zeros_like(total)

    weighted[...] = (phi_rows[0].astype(jnp.float32) * field[0]).astype(jnp.bfloat16)
    for pair in range(owned // 2):
        left = from_ref[tile, 2 * pair]
        right = from_ref[tile, 2 * pair + 1]

        @pl.when(jnp.maximum(left, right) >= 0)
        def _():
            for half, source in enumerate((left, right)):
                start = pl.multiple_of(jnp.maximum(source, 0) * size, size)
                span = pl.ds(start, size)
                values = jnp.where(place_ref[1] == 1, phi_near[0, span, :], phi_far[0, span, :])
                padded[half * size : (half + 1) * size, :] = jnp.where(
                    source >= 0, values, jnp.zeros_like(values)
                )
            product = lax.dot_general(
                weighted[...],
                padded[...],
                (((1,), (1,)), ((), ())),
                preferred_element_type=jnp.float32,
            )
            span = slice(pair * pair_width, (pair + 1) * pair_width)
            for m in range(per_row):
                start = pl.multiple_of(rows_ref[tile, m] * size, size)
                total[pl.ds(start, size), span] += product[m * size : (m + 1) * size]

    @pl.when(tile == pl.num_programs(0) - 1)
    def _():
        step = 4 * size

        @pl.loop(0, total.shape[0] // step)
        def _(chunk):
            for part in range(4):
                span = pl.ds(pl.multiple_of(chunk * step + part * size, size), size)
                out[span, :] = total[span, :] * keep[pl.ds(chunk * 4 + part, 1), :]
            span = pl.ds(pl.multiple_of(chunk * step, step), step)
            terms[span, :] = jnp.dot(
                out[span, :],
                orbitals[...],
                precision=lax.Precision.HIGHEST,
                preferred_element_type=jnp.float32,
            )


def owned_hamiltonian(rows_phi, cols_phi, field, rows, sources, place, keep, orbitals, size, per_column):
    tiles, width, cells = rows_phi.shape
    per_row = rows.shape[1]
    owned = sources.shape[1]
    high = keep.shape[0] * size
    wide = owned * size
    norb = orbitals.shape[1]
    grid_spec = pltpu.PrefetchScalarGridSpec(
        num_scalar_prefetch=3,
        grid=(tiles,),
        in_specs=[
            pl.BlockSpec((1, per_row * size, cells), lambda t, rows, sources, place: (t, 0, 0)),
            pl.BlockSpec(
                (1, per_column * size, cells),
                lambda t, rows, sources, place: (t * place[1], place[0], 0),
            ),
            pl.BlockSpec(
                (1, per_column * size, cells),
                lambda t, rows, sources, place: (t * (1 - place[1]), 0, 0),
            ),
            pl.BlockSpec((1, 1, cells), lambda t, rows, sources, place: (t, 0, 0)),
            pl.BlockSpec(keep.shape, lambda t, rows, sources, place: (0, 0)),
            pl.BlockSpec(orbitals.shape, lambda t, rows, sources, place: (0, 0)),
        ],
        out_specs=[
            pl.BlockSpec((high, wide), lambda t, rows, sources, place: (0, 0)),
            pl.BlockSpec((high, norb), lambda t, rows, sources, place: (0, 0)),
        ],
        scratch_shapes=[
            pltpu.VMEM((high, wide), jnp.float32),
            pltpu.VMEM((per_row * size, cells), jnp.bfloat16),
            pltpu.VMEM((2 * size, cells), jnp.bfloat16),
        ],
    )

    def body(*refs):
        hamiltonian_kernel(per_row, size, owned, *refs)

    return pl.pallas_call(
        body,
        grid_spec=grid_spec,
        out_shape=[
            jax.ShapeDtypeStruct((high, wide), jnp.float32),
            jax.ShapeDtypeStruct((high, norb), jnp.float32),
        ],
        compiler_params=pltpu.CompilerParams(vmem_limit_bytes=vmem_bytes),
        name="owned_hamiltonian",
    )(rows, sources, place, rows_phi, rows_phi, cols_phi, field, keep, orbitals)


def whole_potential(density):
    def difference(values, direction):
        return (jnp.roll(values, -1, direction) - jnp.roll(values, 1, direction)) / (2.0 * spacing)

    gradients = [difference(density, direction) for direction in range(3)]
    grad_square = (
        gradients[0] * gradients[0] + gradients[1] * gradients[1] + gradients[2] * gradients[2]
    )
    first, second = jax.grad(total_energy, argnums=(0, 1))(density, grad_square)
    divergence = sum(
        difference(2.0 * second * gradients[direction], direction) for direction in range(3)
    )
    return first - divergence


def gathered(density_matrix, block_pattern, tile_lists, basis_values, core_density, orbitals):
    row_count = lax.axis_size("row")
    column_count = lax.axis_size("col")
    depth_count = lax.axis_size("gz")
    row_index = lax.axis_index("row")
    column_index = lax.axis_index("col")
    depth_index = lax.axis_index("gz")
    row_blocks, column_blocks = block_pattern.shape
    size = density_matrix.shape[0] // row_blocks
    tiles, listed = tile_lists.shape
    per_row = listed // row_count
    per_column = listed // column_count
    owned = column_blocks // depth_count
    cells = core_density.size
    phi_tile = basis_values.reshape(listed * size, cells)

    lists = tile_lists.reshape(row_count, column_count, depth_count, listed).transpose(2, 0, 1, 3)
    lists = lists.reshape(tiles, listed)
    rows = lax.dynamic_slice_in_dim(lists, row_index * per_row, per_row, 1) - row_index * row_blocks
    cols = (
        lax.dynamic_slice_in_dim(lists, column_index * per_column, per_column, 1)
        - column_index * column_blocks
    )
    slab = row_count * column_count
    slab_rows = lax.dynamic_slice_in_dim(rows, depth_index * slab, slab, 0)
    slab_cols = lax.dynamic_slice_in_dim(cols, depth_index * slab, slab, 0)
    slab_keep = block_pattern[slab_rows[:, :, None], slab_cols[:, None, :]]
    slab_keep = slab_keep.reshape(slab, per_row * per_column)
    half = column_count // row_count
    near = (column_index // half == row_index).astype(jnp.int32)
    place = jnp.stack([column_index % half, near, depth_index * slab]).astype(jnp.int32)
    own_ids = depth_index * owned + jnp.arange(owned, dtype=jnp.int32)
    matches = cols[:, None, :] == own_ids[None, :, None]
    numbers = jnp.arange(per_column, dtype=jnp.int32)[None, None, :]
    sources = jnp.max(jnp.where(matches, numbers, -1), axis=2).astype(jnp.int32)
    own_pattern = lax.dynamic_slice_in_dim(block_pattern, depth_index * owned, owned, 1)
    keep = jnp.repeat(own_pattern.astype(jnp.float32), size, axis=1)

    rows_phi, cols_phi = gather_basis(phi_tile, row_count, column_count, depth_count)
    partial = partial_density(
        density_matrix, rows_phi, cols_phi, slab_rows, slab_cols, slab_keep, place, size
    )
    partial = partial.reshape(slab, cells)
    own_tile = (row_index * column_count + column_index) == jnp.arange(slab)[:, None]
    partial = partial + jnp.where(own_tile, core_density.reshape(1, cells), 0.0)
    parts = sum_density(partial, row_count, column_count, depth_count)
    tile_shape = core_density.shape
    grid = parts.reshape((depth_count, row_count, column_count) + tile_shape)
    grid = grid.transpose(1, 3, 2, 4, 0, 5).reshape(
        row_count * tile_shape[0], column_count * tile_shape[1], depth_count * tile_shape[2]
    )
    field = whole_potential(jnp.maximum(grid, density_floor))
    field = field.reshape(
        row_count, tile_shape[0], column_count, tile_shape[1], depth_count, tile_shape[2]
    )
    field = field.transpose(4, 0, 2, 1, 3, 5).reshape(tiles, 1, cells)
    hamiltonian, terms = owned_hamiltonian(
        rows_phi, cols_phi, field, rows, sources, place, keep, orbitals, size, per_column
    )
    applied = sum_applied(terms, column_count)
    return hamiltonian, applied


def shards(density_matrix, block_pattern, tile_lists, basis_values, core_density, orbitals):
    arguments = (
        density_matrix, block_pattern, tile_lists, basis_values, core_density, orbitals,
    )
    counts = lax.axis_size("row"), lax.axis_size("col"), lax.axis_size("gz")
    fits = tile_lists.shape[0] * basis_values.size * 2 <= gathered_limit
    fits = fits and counts[0] == 2 and counts[1] % 2 == 0 and counts[2] == 4
    return gathered(*arguments) if fits else exchanged(*arguments)


def solution(mesh):
    placed = (
        P("row", "col"),
        P("row", "col"),
        P(),
        P("row", "col", "gz", None, None),
        P("row", "col", "gz"),
        P(("col", "gz"), None),
    )
    return jax.shard_map(
        shards,
        mesh=mesh,
        in_specs=placed,
        out_specs=(P("row", ("col", "gz")), P(("row", "col", "gz"), None)),
        check_vma=False,
    )
```

```python
import jax
import jax.numpy as jnp
from jax import lax
from jax.experimental import pallas as pl
from jax.experimental.pallas import tpu as pltpu
from jax.sharding import PartitionSpec as P

pbe_kappa = 0.804
pbe_mu = 0.2195149727645171
exch_const = 0.75 * (3.0 / 3.141592653589793) ** (1.0 / 3.0)
grad_scale = 4.0 * (3.0 * 3.141592653589793**2) ** (2.0 / 3.0)
density_floor = 0.2
spacing = 0.125


def with_halo(cells, sides, width):
    for axis, dim in sides:
        count = lax.axis_size(axis)
        head = lax.slice_in_dim(cells, 0, width, axis=dim)
        tail = lax.slice_in_dim(cells, cells.shape[dim] - width, cells.shape[dim], axis=dim)
        cells = jnp.concatenate(
            [
                lax.ppermute(tail, axis, [(i, (i + 1) % count) for i in range(count)]),
                cells,
                lax.ppermute(head, axis, [((i + 1) % count, i) for i in range(count)]),
            ],
            axis=dim,
        )
    return cells


def energy(density, grad_square):
    scaled = grad_square / (grad_scale * density ** (8.0 / 3.0))
    enhance = 1.0 + pbe_kappa - pbe_kappa / (1.0 + pbe_mu * scaled / pbe_kappa)
    return -exch_const * density ** (4.0 / 3.0) * enhance


def total_energy(density, grad_square):
    return jnp.sum(energy(density, grad_square))


def centered(grid_values, direction):
    higher = [slice(1, -1), slice(1, -1), slice(1, -1)]
    lesser = [slice(1, -1), slice(1, -1), slice(1, -1)]
    higher[direction] = slice(2, None)
    lesser[direction] = slice(None, -2)
    return (grid_values[tuple(higher)] - grid_values[tuple(lesser)]) / (2.0 * spacing)


def potential_twice(density):
    padded = with_halo(density, (("row", 0), ("col", 1), ("gz", 2)), 1)
    gradients = [centered(padded, direction) for direction in range(3)]
    grad_square = (
        gradients[0] * gradients[0] + gradients[1] * gradients[1] + gradients[2] * gradients[2]
    )
    first, second = jax.grad(total_energy, argnums=(0, 1))(density, grad_square)
    fluxes = jnp.stack([2.0 * second * gradients[direction] for direction in range(3)])
    flux_ext = with_halo(fluxes, (("row", 1), ("col", 2), ("gz", 3)), 1)
    divergence = centered(flux_ext[0], 0) + centered(flux_ext[1], 1) + centered(flux_ext[2], 2)
    return first - divergence


def exchanged(density_matrix, block_pattern, tile_lists, basis_values, core_density, orbitals):
    row_count = lax.axis_size("row")
    column_count = lax.axis_size("col")
    depth_count = lax.axis_size("gz")
    row_index = lax.axis_index("row")
    column_index = lax.axis_index("col")
    depth_index = lax.axis_index("gz")
    row_blocks, column_blocks = block_pattern.shape
    block_size = density_matrix.shape[0] // row_blocks
    listed = tile_lists.shape[1]
    per_row = listed // row_count
    per_column = listed // column_count
    width = listed * block_size
    block_area = block_size * block_size
    slab_lists = tile_lists.reshape(row_count, column_count, depth_count, listed)
    slab_lists = lax.dynamic_index_in_dim(slab_lists, depth_index, axis=2, keepdims=False)
    mine_rows = (
        lax.dynamic_slice_in_dim(slab_lists, row_index * per_row, per_row, 2)
        - row_index * row_blocks
    )
    mine_cols = (
        lax.dynamic_slice_in_dim(slab_lists, column_index * per_column, per_column, 2)
        - column_index * column_blocks
    )
    block_ids = (mine_rows[:, :, :, None] * column_blocks + mine_cols[:, :, None, :]).reshape(-1)
    pattern_flat = block_pattern.reshape(-1)
    stored = density_matrix.reshape(row_blocks, block_size, column_blocks, block_size)
    stored = stored.transpose(0, 2, 1, 3).reshape(row_blocks * column_blocks, block_area)
    stored = stored * pattern_flat.astype(jnp.bfloat16)[:, None]
    outgoing = jnp.take(stored, block_ids, axis=0).reshape(
        row_count, column_count, per_row * per_column, block_area
    )
    flat_out = outgoing.reshape(row_count * column_count, per_row * per_column, block_area)
    incoming = lax.all_to_all(flat_out, ("row", "col"), split_axis=0, concat_axis=0, tiled=True)
    tile_matrix = incoming.reshape(
        row_count, column_count, per_row, per_column, block_size, block_size
    )
    tile_matrix = tile_matrix.transpose(0, 2, 4, 1, 3, 5).reshape(width, width)
    phi_tile = basis_values.reshape(width, -1)
    product = jnp.dot(tile_matrix, phi_tile, preferred_element_type=jnp.float32)
    rho_tile = jnp.sum(phi_tile * product, axis=0).reshape(core_density.shape)
    density = jnp.maximum(rho_tile + core_density, density_floor)
    field = potential_twice(density)
    weighted = (phi_tile * field.reshape(1, -1)).astype(jnp.bfloat16)
    local_ham = lax.dot_general(
        weighted, phi_tile, (((1,), (1,)), ((), ())), preferred_element_type=jnp.float32
    )
    returning = local_ham.reshape(
        row_count, per_row, block_size, column_count, per_column, block_size
    )
    returning = returning.transpose(0, 3, 1, 4, 2, 5).reshape(
        row_count, column_count, per_row * per_column, block_area
    )
    flat_back = returning.reshape(row_count * column_count, per_row * per_column, block_area)
    arrived = lax.all_to_all(flat_back, ("row", "col"), split_axis=0, concat_axis=0, tiled=True)
    owned = jnp.zeros((row_blocks * column_blocks, block_area), jnp.float32)
    owned = owned.at[block_ids].add(arrived.reshape(-1, block_area))
    owned = owned * pattern_flat.astype(jnp.float32)[:, None]
    dense = owned.reshape(row_blocks, column_blocks, block_size, block_size)
    dense = dense.transpose(0, 2, 1, 3).reshape(row_blocks * block_size, column_blocks * block_size)
    share = lax.psum_scatter(dense, "gz", scatter_dimension=1, tiled=True)
    terms = jnp.dot(
        share, orbitals, precision=lax.Precision.HIGHEST, preferred_element_type=jnp.float32
    )
    applied = lax.psum_scatter(terms, ("col", "gz"), scatter_dimension=0, tiled=True)
    return (share, applied)


vmem_bytes = 56 * 1024 * 1024
gathered_limit = 48 * 1024 * 1024


MESH = pl.DeviceIdType.MESH


def meet(peers):
    barrier = pltpu.get_barrier_semaphore()
    for peer in peers:
        pl.semaphore_signal(barrier, inc=1, device_id=peer, device_id_type=MESH)
    pl.semaphore_wait(barrier, len(peers))


def basis_kernel(row_count, column_count, phi, rows_out, cols_out, own_sem, send, got, got_cols):
    i, j, k = lax.axis_index("row"), lax.axis_index("col"), lax.axis_index("gz")
    across = 1 - i
    beside = lax.rem(k + 2, 4)
    twin = k + 1 - 2 * lax.rem(k, 2)
    half = column_count // row_count
    share = phi.shape[1] // half
    provider = (j // half) == i
    offset = pl.multiple_of(lax.rem(j, half) * share, share)
    x_peer, y_peer, c_peer = (across, j, k), (i, j, beside), (i, j, twin)
    up, down = lax.rem(j + 1, column_count), lax.rem(j + column_count - 1, column_count)
    z_up, z_down = (i, up, k), (i, down, k)
    meet([x_peer, y_peer, c_peer, z_up, z_down])
    has_up, has_down = j < column_count - 1, j > 0
    started, started_cols, started_twin, guarded = [], [], [], []

    def push(source, target, arrival, peer, log):
        number = len(started) + len(started_cols) + len(started_twin) + len(guarded)
        copy = pltpu.make_async_remote_copy(
            src_ref=source, dst_ref=target, send_sem=send.at[number], recv_sem=arrival,
            device_id=peer, device_id_type=MESH,
        )
        log.append(copy)
        return copy

    def arrived(out, sems, where):
        pltpu.make_async_remote_copy(
            src_ref=out.at[where], dst_ref=out.at[where], send_sem=send.at[0],
            recv_sem=sems.at[where], device_id=x_peer, device_id_type=MESH,
        ).wait_recv()

    own = (k, i, j)
    local = pltpu.make_async_copy(phi.at[i], rows_out.at[own], own_sem)
    local.start()
    push(phi.at[across], rows_out.at[own], got.at[own], x_peer, started).start()

    queue = []

    sent_z = []

    def along(source, where, peer, condition):
        copy = push(source, rows_out.at[where], got.at[where], peer, guarded)
        sent_z.append((copy, condition))
        pl.when(condition)(copy.start)

    def spread(source, where, along_y):
        if along_y:
            push(source, rows_out.at[where], got.at[where], y_peer, started).start()
        column = push(
            source.at[pl.ds(offset, share)], cols_out.at[where], got_cols.at[where], x_peer,
            started_cols,
        )
        pl.when(provider)(column.start)
        push(source, rows_out.at[where], got.at[where], c_peer, started).start()
        queue.append(where)
        if len(queue) > 3:
            relay(queue.pop(0))

    def relay(where):
        copy = push(
            cols_out.at[where], cols_out.at[where], got_cols.at[where], c_peer, started_twin
        )

        @pl.when(jnp.logical_not(provider))
        def _():
            arrived(cols_out, got_cols, where)
            copy.start()

    along(phi.at[i], own, z_up, has_up)
    along(phi.at[i], own, z_down, has_down)
    spread(phi.at[i], own, True)
    where = (k, across, j)
    arrived(rows_out, got, where)
    along(rows_out.at[where], where, z_up, has_up)
    along(rows_out.at[where], where, z_down, has_down)
    spread(rows_out.at[where], where, True)
    order = []
    for step in range(1, column_count):
        low, high = jnp.minimum(j, column_count - 1 - j), column_count - 1
        turn = (step + 1) // 2
        both = turn <= low
        sign_down = step % 2 == 1
        paired = j - turn if sign_down else j + turn
        rest = jnp.where(j < column_count - 1 - j, j + (step - low), j - (step - low))
        order.append(jnp.where(both, paired, rest))
    for other in order:
        for side in (i, across):
            where = (k, side, other)
            arrived(rows_out, got, where)
            along(rows_out.at[where], where, z_up, jnp.logical_and(other < j, has_up))
            along(rows_out.at[where], where, z_down, jnp.logical_and(other > j, has_down))
            spread(rows_out.at[where], where, True)
    slab = [(side, other) for other in order for side in (i, across)]
    for side, other in [(i, j), (across, j)] + slab:
        where = (beside, side, other)
        arrived(rows_out, got, where)
        spread(rows_out.at[where], where, False)
    while queue:
        relay(queue.pop(0))
    for depth in (twin, lax.rem(twin + 2, 4)):
        for side, other in [(i, j), (across, j)] + slab:
            arrived(rows_out, got, (depth, side, other))

    @pl.when(jnp.logical_not(provider))
    def _():
        for depth in (twin, lax.rem(twin + 2, 4)):
            for side, other in [(i, j), (across, j)] + slab:
                arrived(cols_out, got_cols, (depth, side, other))
        for copy in started_twin:
            copy.wait_send()

    @pl.when(provider)
    def _():
        for copy in started_cols:
            copy.wait_send()

    for copy in started:
        copy.wait_send()
    for copy, condition in sent_z:
        pl.when(condition)(copy.wait_send)
    local.wait()


def gather_basis(phi_tile, row_count, column_count, depth_count):
    width, cells = phi_tile.shape
    halves = phi_tile.reshape(row_count, width // row_count, cells)
    grid = (depth_count, row_count, column_count)
    count = row_count * column_count
    messages = 1 + 3 * count + 3 * 2 * count

    def body(*refs):
        basis_kernel(row_count, column_count, *refs)

    rows_phi, cols_phi = pl.pallas_call(
        body,
        in_specs=[pl.BlockSpec(memory_space=pltpu.HBM)],
        out_specs=[pl.BlockSpec(memory_space=pltpu.HBM)] * 2,
        out_shape=[
            jax.ShapeDtypeStruct(grid + (width // row_count, cells), phi_tile.dtype),
            jax.ShapeDtypeStruct(grid + (width // column_count, cells), phi_tile.dtype),
        ],
        scratch_shapes=[
            pltpu.SemaphoreType.DMA,
            pltpu.SemaphoreType.DMA((messages,)),
            pltpu.SemaphoreType.DMA(grid),
            pltpu.SemaphoreType.DMA(grid),
        ],
        compiler_params=pltpu.CompilerParams(collective_id=0, has_side_effects=True),
        name="gather_basis",
    )(halves)
    tiles = depth_count * count
    return (
        rows_phi.reshape(tiles, width // row_count, cells),
        cols_phi.reshape(tiles, width // column_count, cells),
    )


def sum_kernel(row_count, column_count, depth_count, partial, out, slots, slabs, send, got, got_slab):
    i, j, k = lax.axis_index("row"), lax.axis_index("col"), lax.axis_index("gz")
    count = row_count * column_count
    me = i * column_count + j
    peers = [lax.rem(me + step, count) for step in range(1, count)]
    depths = [lax.rem(k + step, depth_count) for step in range(1, depth_count)]
    ids = [(peer // column_count, lax.rem(peer, column_count), k) for peer in peers]
    depth_ids = [(i, j, depth) for depth in depths]
    meet(ids + depth_ids)
    copies = []
    for number, peer in enumerate(ids):
        copy = pltpu.make_async_remote_copy(
            src_ref=partial, dst_ref=slots.at[me], send_sem=send.at[number],
            recv_sem=got.at[me], device_id=peer, device_id_type=MESH,
        )
        copy.start()
        copies.append(copy)
    slots[me] = partial[...]
    for peer in peers:
        pltpu.make_async_remote_copy(
            src_ref=partial, dst_ref=slots.at[peer], send_sem=send.at[0],
            recv_sem=got.at[peer], device_id=ids[0], device_id_type=MESH,
        ).wait_recv()
    summed = slots[0]
    for number in range(1, count):
        summed = summed + slots[number]
    slabs[k] = summed
    for number, peer in enumerate(depth_ids):
        copy = pltpu.make_async_remote_copy(
            src_ref=slabs.at[k], dst_ref=slabs.at[k], send_sem=send.at[count - 1 + number],
            recv_sem=got_slab.at[k], device_id=peer, device_id_type=MESH,
        )
        copy.start()
        copies.append(copy)
    for depth in depths:
        pltpu.make_async_remote_copy(
            src_ref=partial, dst_ref=slabs.at[depth], send_sem=send.at[0],
            recv_sem=got_slab.at[depth], device_id=ids[0], device_id_type=MESH,
        ).wait_recv()
    out[...] = slabs[...]
    for copy in copies:
        copy.wait_send()


def sum_density(partial, row_count, column_count, depth_count):
    count = row_count * column_count

    def body(*refs):
        sum_kernel(row_count, column_count, depth_count, *refs)

    return pl.pallas_call(
        body,
        in_specs=[pl.BlockSpec(memory_space=pltpu.VMEM)],
        out_specs=pl.BlockSpec(memory_space=pltpu.VMEM),
        out_shape=jax.ShapeDtypeStruct((depth_count,) + partial.shape, partial.dtype),
        scratch_shapes=[
            pltpu.VMEM((count,) + partial.shape, partial.dtype),
            pltpu.VMEM((depth_count,) + partial.shape, partial.dtype),
            pltpu.SemaphoreType.DMA((count + depth_count,)),
            pltpu.SemaphoreType.DMA((count,)),
            pltpu.SemaphoreType.DMA((depth_count,)),
        ],
        compiler_params=pltpu.CompilerParams(collective_id=1, has_side_effects=True),
        name="sum_density",
    )(partial)


def applied_kernel(column_count, terms, out, c_got, y_send, y_got, z_send, z_got, send, got):
    i, j, k = lax.axis_index("row"), lax.axis_index("col"), lax.axis_index("gz")
    y, c = k // 2, lax.rem(k, 2)
    y_peer, c_peer = (i, j, lax.rem(k + 2, 4)), (i, j, k + 1 - 2 * c)
    others = [lax.rem(j + step, column_count) for step in range(1, column_count)]
    z_peers = [(i, other, k) for other in others]
    meet([y_peer, c_peer] + z_peers)

    def push(number, source, target, peer):
        copy = pltpu.make_async_remote_copy(
            src_ref=source, dst_ref=target, send_sem=send.at[number], recv_sem=got.at[number],
            device_id=peer, device_id_type=MESH,
        )
        copy.start()
        return copy

    first = push(0, terms.at[1 - y, 1 - c], c_got.at[0], c_peer)
    second = push(1, terms.at[y, 1 - c], c_got.at[1], c_peer)
    first.wait_recv()
    y_send[...] = terms[1 - y, c] + c_got[0]
    third = push(2, y_send, y_got, y_peer)
    second.wait_recv()
    z_send[...] = terms[y, c] + c_got[1]
    third.wait_recv()
    z_send[...] = z_send[...] + y_got[...]
    last = []
    for number, (other, peer) in enumerate(zip(others, z_peers)):
        last.append(push(3 + number, z_send.at[other], z_got.at[number], peer))
    total = z_send[j]
    for number, copy in enumerate(last):
        copy.wait_recv()
        total = total + z_got[number]
    out[...] = total
    for copy in [first, second, third] + last:
        copy.wait_send()


def sum_applied(terms, column_count):
    rows, norb = terms.shape[3:]
    part = (column_count, rows, norb)

    def body(*refs):
        applied_kernel(column_count, *refs)

    return pl.pallas_call(
        body,
        in_specs=[pl.BlockSpec(memory_space=pltpu.VMEM)],
        out_specs=pl.BlockSpec(memory_space=pltpu.VMEM),
        out_shape=jax.ShapeDtypeStruct((rows, norb), terms.dtype),
        scratch_shapes=[
            pltpu.VMEM((2,) + part, terms.dtype),
            pltpu.VMEM(part, terms.dtype),
            pltpu.VMEM(part, terms.dtype),
            pltpu.VMEM(part, terms.dtype),
            pltpu.VMEM((column_count - 1, rows, norb), terms.dtype),
            pltpu.SemaphoreType.DMA((2 + column_count,)),
            pltpu.SemaphoreType.DMA((2 + column_count,)),
        ],
        compiler_params=pltpu.CompilerParams(
            collective_id=2, has_side_effects=True, vmem_limit_bytes=vmem_bytes // 2
        ),
        name="sum_applied",
    )(terms)


def density_kernel(per_row, per_column, size, counts, lists_ref, pattern_ref, place_ref, *refs):
    strips = refs[:per_row]
    phi_rows, phi_near, phi_far, out, picked, padded = refs[per_row:]
    pair_width = 2 * size
    row_blocks, column_blocks = pattern_ref.shape
    tile = pl.program_id(0) * counts[2] + place_ref[5]
    rows = [lists_ref[tile, place_ref[3] * per_row + m] for m in range(per_row)]
    rows = [row - place_ref[3] * row_blocks for row in rows]
    for n in range(per_column):
        column = lists_ref[tile, place_ref[4] * per_column + n] - place_ref[4] * column_blocks
        start = pl.multiple_of((column // 2) * pair_width, pair_width)
        odd = column % 2
        span = slice(n * size, (n + 1) * size)
        values = jnp.where(place_ref[1] == 1, phi_near[0, span, :], phi_far[0, span, :])
        for half in range(2):
            padded[n * pair_width + half * size : n * pair_width + (half + 1) * size, :] = (
                jnp.where(odd == half, values, jnp.zeros_like(values))
            )
        for m in range(per_row):
            block = strips[m][:, pl.ds(start, pair_width)]
            kept = pattern_ref[rows[m], column] != 0
            picked[m * size : (m + 1) * size, n * pair_width : (n + 1) * pair_width] = jnp.where(
                kept, block, jnp.zeros_like(block)
            )
    product = jnp.dot(picked[...], padded[...], preferred_element_type=jnp.float32)
    rho = jnp.sum(phi_rows[0].astype(jnp.float32) * product, axis=0, keepdims=True)
    out[0] = rho


def partial_density(density_matrix, rows_phi, cols_phi, lists, pattern, place, size, counts):
    tiles, cells = counts[0] * counts[1], rows_phi.shape[2]
    per_row, per_column = lists.shape[1] // counts[0], lists.shape[1] // counts[1]
    row_blocks = pattern.shape[0]
    columns = density_matrix.shape[1]

    def strip_spec(m):
        def strip(t, lists, pattern, place):
            row = lists[t * counts[2] + place[5], place[3] * per_row + m]
            return row - place[3] * row_blocks, 0

        return pl.BlockSpec((size, columns), strip)

    grid_spec = pltpu.PrefetchScalarGridSpec(
        num_scalar_prefetch=3,
        grid=(tiles,),
        in_specs=[strip_spec(m) for m in range(per_row)]
        + [
            pl.BlockSpec(
                (1, per_row * size, cells),
                lambda t, lists, pattern, place: (place[2] + t, 0, 0),
            ),
            pl.BlockSpec(
                (1, per_column * size, cells),
                lambda t, lists, pattern, place: ((place[2] + t) * place[1], place[0], 0),
            ),
            pl.BlockSpec(
                (1, per_column * size, cells),
                lambda t, lists, pattern, place: ((place[2] + t) * (1 - place[1]), 0, 0),
            ),
        ],
        out_specs=pl.BlockSpec((1, 1, cells), lambda t, lists, pattern, place: (t, 0, 0)),
        scratch_shapes=[
            pltpu.VMEM((per_row * size, 2 * per_column * size), jnp.bfloat16),
            pltpu.VMEM((2 * per_column * size, cells), jnp.bfloat16),
        ],
    )

    def body(*refs):
        density_kernel(per_row, per_column, size, counts, *refs)

    return pl.pallas_call(
        body,
        grid_spec=grid_spec,
        out_shape=jax.ShapeDtypeStruct((tiles, 1, cells), jnp.float32),
        compiler_params=pltpu.CompilerParams(vmem_limit_bytes=vmem_bytes),
        cost_estimate=pl.CostEstimate(
            flops=4 * tiles * per_row * per_column * size * size * cells,
            bytes_accessed=tiles * per_row * size * columns * 2,
            transcendentals=0,
        ),
        name="partial_density",
    )(lists, pattern, place, *([density_matrix] * per_row), rows_phi, rows_phi, cols_phi)


def hamiltonian_kernel(
    per_row, per_column, size, owned, counts, together, column_blocks, lists_ref, place_ref,
    phi_rows, phi_near, phi_far, field, keep, upper, lower, out, terms, total, weighted, padded,
    sems,
):
    step = pl.program_id(0)
    pair_width = 2 * size
    slab = counts[0] * counts[1]
    row_blocks = total.shape[0] // size

    @pl.when(step == 0)
    def _():
        total[...] = jnp.zeros_like(total)

    for inner in range(together):
        number = step * together + inner
        tile = lax.rem(number, slab) * counts[2] + number // slab
        base = place_ref[4] * column_blocks + place_ref[5] * owned
        listed = [lists_ref[tile, place_ref[4] * per_column + n] - base for n in range(per_column)]
        weighted[...] = (phi_rows[inner].astype(jnp.float32) * field[inner]).astype(jnp.bfloat16)
        for pair in range(owned // 2):
            sources = []
            for half in range(2):
                source = jnp.int32(-1)
                for n in range(per_column):
                    source = jnp.where(listed[n] == 2 * pair + half, n, source)
                sources.append(source)

            @pl.when(jnp.maximum(sources[0], sources[1]) >= 0)
            def _():
                for half, source in enumerate(sources):
                    span = pl.ds(pl.multiple_of(jnp.maximum(source, 0) * size, size), size)
                    values = jnp.where(
                        place_ref[1] == 1, phi_near[inner, span, :], phi_far[inner, span, :]
                    )
                    padded[half * size : (half + 1) * size, :] = jnp.where(
                        source >= 0, values, jnp.zeros_like(values)
                    )
                product = lax.dot_general(
                    weighted[...],
                    padded[...],
                    (((1,), (1,)), ((), ())),
                    preferred_element_type=jnp.float32,
                )
                span = slice(pair * pair_width, (pair + 1) * pair_width)
                for m in range(per_row):
                    row = lists_ref[tile, place_ref[3] * per_row + m] - place_ref[3] * row_blocks
                    start = pl.multiple_of(row * size, size)
                    total[pl.ds(start, size), span] += product[m * size : (m + 1) * size]

    @pl.when(step == pl.num_programs(0) - 1)
    def _():
        high = terms.shape[3]
        parts = high // size
        copies = []
        norb = lower.shape[1]
        for chunk in range(total.shape[0] // high):
            for part in range(parts):
                block = chunk * parts + part
                span = slice(block * size, (block + 1) * size)
                total[span, :] = total[span, :] * keep[block : block + 1, :]
            span = slice(chunk * high, (chunk + 1) * high)
            copy = pltpu.make_async_copy(total.at[span], out.at[span], sems.at[chunk])
            copy.start()
            copies.append(copy)
            values = total[span, :]
            coarse = values.astype(jnp.bfloat16)
            fine = (values - coarse.astype(jnp.float32)).astype(jnp.bfloat16)
            first = jnp.dot(coarse, upper[...], preferred_element_type=jnp.float32)
            second = jnp.dot(fine, upper[:, :norb], preferred_element_type=jnp.float32)
            depth = chunk % counts[2]
            terms[depth // 2, depth % 2, chunk // counts[2]] = (
                first[:, :norb] + (first[:, norb:] + second)
            )
        for copy in copies:
            copy.wait()


def owned_hamiltonian(rows_phi, cols_phi, field, lists, place, keep, orbitals, size, counts):
    tiles, width, cells = rows_phi.shape
    per_row, per_column = lists.shape[1] // counts[0], lists.shape[1] // counts[1]
    high = keep.shape[0] * size
    wide = keep.shape[1]
    owned = wide // size
    norb = orbitals.shape[1]
    together = 4
    chunks = counts[1] * counts[2]
    rounded = lax.reduce_precision(orbitals, exponent_bits=8, mantissa_bits=7)
    coarse = rounded.astype(jnp.bfloat16)
    fine = (orbitals - rounded).astype(jnp.bfloat16)
    upper = jnp.concatenate([coarse, fine], axis=1)
    term_shape = (2, 2, counts[1], high // chunks, norb)
    grid_spec = pltpu.PrefetchScalarGridSpec(
        num_scalar_prefetch=2,
        grid=(tiles // together,),
        in_specs=[
            pl.BlockSpec((together, per_row * size, cells), lambda t, lists, place: (t, 0, 0)),
            pl.BlockSpec(
                (together, per_column * size, cells),
                lambda t, lists, place: (t * place[1], place[0], 0),
            ),
            pl.BlockSpec(
                (together, per_column * size, cells),
                lambda t, lists, place: (t * (1 - place[1]), 0, 0),
            ),
            pl.BlockSpec((together, 1, cells), lambda t, lists, place: (t, 0, 0)),
            pl.BlockSpec(keep.shape, lambda t, lists, place: (0, 0)),
            pl.BlockSpec(upper.shape, lambda t, lists, place: (0, 0)),
            pl.BlockSpec(coarse.shape, lambda t, lists, place: (0, 0)),
        ],
        out_specs=[
            pl.BlockSpec(memory_space=pltpu.HBM),
            pl.BlockSpec(term_shape, lambda t, lists, place: (0, 0, 0, 0, 0)),
        ],
        scratch_shapes=[
            pltpu.VMEM((high, wide), jnp.float32),
            pltpu.VMEM((per_row * size, cells), jnp.bfloat16),
            pltpu.VMEM((2 * size, cells), jnp.bfloat16),
            pltpu.SemaphoreType.DMA((chunks,)),
        ],
    )

    def body(*refs):
        hamiltonian_kernel(
            per_row, per_column, size, owned, counts, together, owned * counts[2], *refs
        )

    return pl.pallas_call(
        body,
        grid_spec=grid_spec,
        out_shape=[
            jax.ShapeDtypeStruct((high, wide), jnp.float32),
            jax.ShapeDtypeStruct(term_shape, jnp.float32),
        ],
        compiler_params=pltpu.CompilerParams(vmem_limit_bytes=vmem_bytes),
        name="owned_hamiltonian",
    )(lists, place, rows_phi, rows_phi, cols_phi, field, keep, upper, coarse)


def whole_potential(density):
    def difference(values, direction):
        return (jnp.roll(values, -1, direction) - jnp.roll(values, 1, direction)) / (2.0 * spacing)

    gradients = [difference(density, direction) for direction in range(3)]
    grad_square = (
        gradients[0] * gradients[0] + gradients[1] * gradients[1] + gradients[2] * gradients[2]
    )
    first, second = jax.grad(total_energy, argnums=(0, 1))(density, grad_square)
    divergence = sum(
        difference(2.0 * second * gradients[direction], direction) for direction in range(3)
    )
    return first - divergence


def gathered(density_matrix, block_pattern, tile_lists, basis_values, core_density, orbitals):
    row_count = lax.axis_size("row")
    column_count = lax.axis_size("col")
    depth_count = lax.axis_size("gz")
    row_index = lax.axis_index("row")
    column_index = lax.axis_index("col")
    depth_index = lax.axis_index("gz")
    row_blocks, column_blocks = block_pattern.shape
    size = density_matrix.shape[0] // row_blocks
    tiles, listed = tile_lists.shape
    owned = column_blocks // depth_count
    cells = core_density.size
    phi_tile = basis_values.reshape(listed * size, cells)

    slab = row_count * column_count
    counts = (row_count, column_count, depth_count)
    half = column_count // row_count
    near = (column_index // half == row_index).astype(jnp.int32)
    place = [column_index % half, near, depth_index * slab, row_index, column_index, depth_index]
    place = jnp.stack(place).astype(jnp.int32)
    own_pattern = lax.dynamic_slice_in_dim(block_pattern, depth_index * owned, owned, 1)
    keep = jnp.repeat(own_pattern.astype(jnp.float32), size, axis=1)

    rows_phi, cols_phi = gather_basis(phi_tile, row_count, column_count, depth_count)
    partial = partial_density(
        density_matrix, rows_phi, cols_phi, tile_lists, block_pattern, place, size, counts
    )
    partial = partial.reshape(slab, cells)
    own_tile = (row_index * column_count + column_index) == jnp.arange(slab)[:, None]
    partial = partial + jnp.where(own_tile, core_density.reshape(1, cells), 0.0)
    parts = sum_density(partial, row_count, column_count, depth_count)
    tile_shape = core_density.shape
    grid = parts.reshape((depth_count, row_count, column_count) + tile_shape)
    grid = grid.transpose(1, 3, 2, 4, 0, 5).reshape(
        row_count * tile_shape[0], column_count * tile_shape[1], depth_count * tile_shape[2]
    )
    field = whole_potential(jnp.maximum(grid, density_floor))
    field = field.reshape(
        row_count, tile_shape[0], column_count, tile_shape[1], depth_count, tile_shape[2]
    )
    field = field.transpose(4, 0, 2, 1, 3, 5).reshape(tiles, 1, cells)
    hamiltonian, terms = owned_hamiltonian(
        rows_phi, cols_phi, field, tile_lists, place, keep, orbitals, size, counts
    )
    applied = sum_applied(terms, column_count)
    return hamiltonian, applied


def shards(density_matrix, block_pattern, tile_lists, basis_values, core_density, orbitals):
    arguments = (
        density_matrix, block_pattern, tile_lists, basis_values, core_density, orbitals,
    )
    counts = lax.axis_size("row"), lax.axis_size("col"), lax.axis_size("gz")
    fits = tile_lists.shape[0] * basis_values.size * 2 <= gathered_limit
    fits = fits and counts[0] == 2 and counts[1] % 2 == 0 and counts[2] == 4
    return gathered(*arguments) if fits else exchanged(*arguments)


def solution(mesh):
    placed = (
        P("row", "col"),
        P("row", "col"),
        P(),
        P("row", "col", "gz", None, None),
        P("row", "col", "gz"),
        P(("col", "gz"), None),
    )
    return jax.shard_map(
        shards,
        mesh=mesh,
        in_specs=placed,
        out_specs=(P("row", ("col", "gz")), P(("row", "col", "gz"), None)),
        check_vma=False,
    )
```

```python
import jax
import jax.numpy as jnp
from jax import lax
from jax.experimental import pallas as pl
from jax.experimental.pallas import tpu as pltpu
from jax.sharding import PartitionSpec as P

pbe_kappa = 0.804
pbe_mu = 0.2195149727645171
exch_const = 0.75 * (3.0 / 3.141592653589793) ** (1.0 / 3.0)
grad_scale = 4.0 * (3.0 * 3.141592653589793**2) ** (2.0 / 3.0)
density_floor = 0.2
spacing = 0.125


def with_halo(cells, sides, width):
    for axis, dim in sides:
        count = lax.axis_size(axis)
        head = lax.slice_in_dim(cells, 0, width, axis=dim)
        tail = lax.slice_in_dim(cells, cells.shape[dim] - width, cells.shape[dim], axis=dim)
        cells = jnp.concatenate(
            [
                lax.ppermute(tail, axis, [(i, (i + 1) % count) for i in range(count)]),
                cells,
                lax.ppermute(head, axis, [((i + 1) % count, i) for i in range(count)]),
            ],
            axis=dim,
        )
    return cells


def energy(density, grad_square):
    scaled = grad_square / (grad_scale * density ** (8.0 / 3.0))
    enhance = 1.0 + pbe_kappa - pbe_kappa / (1.0 + pbe_mu * scaled / pbe_kappa)
    return -exch_const * density ** (4.0 / 3.0) * enhance


def total_energy(density, grad_square):
    return jnp.sum(energy(density, grad_square))


def centered(grid_values, direction):
    higher = [slice(1, -1), slice(1, -1), slice(1, -1)]
    lesser = [slice(1, -1), slice(1, -1), slice(1, -1)]
    higher[direction] = slice(2, None)
    lesser[direction] = slice(None, -2)
    return (grid_values[tuple(higher)] - grid_values[tuple(lesser)]) / (2.0 * spacing)


def potential_twice(density):
    padded = with_halo(density, (("row", 0), ("col", 1), ("gz", 2)), 1)
    gradients = [centered(padded, direction) for direction in range(3)]
    grad_square = (
        gradients[0] * gradients[0] + gradients[1] * gradients[1] + gradients[2] * gradients[2]
    )
    first, second = jax.grad(total_energy, argnums=(0, 1))(density, grad_square)
    fluxes = jnp.stack([2.0 * second * gradients[direction] for direction in range(3)])
    flux_ext = with_halo(fluxes, (("row", 1), ("col", 2), ("gz", 3)), 1)
    divergence = centered(flux_ext[0], 0) + centered(flux_ext[1], 1) + centered(flux_ext[2], 2)
    return first - divergence


def exchanged(density_matrix, block_pattern, tile_lists, basis_values, core_density, orbitals):
    row_count = lax.axis_size("row")
    column_count = lax.axis_size("col")
    depth_count = lax.axis_size("gz")
    row_index = lax.axis_index("row")
    column_index = lax.axis_index("col")
    depth_index = lax.axis_index("gz")
    row_blocks, column_blocks = block_pattern.shape
    block_size = density_matrix.shape[0] // row_blocks
    listed = tile_lists.shape[1]
    per_row = listed // row_count
    per_column = listed // column_count
    width = listed * block_size
    block_area = block_size * block_size
    slab_lists = tile_lists.reshape(row_count, column_count, depth_count, listed)
    slab_lists = lax.dynamic_index_in_dim(slab_lists, depth_index, axis=2, keepdims=False)
    mine_rows = (
        lax.dynamic_slice_in_dim(slab_lists, row_index * per_row, per_row, 2)
        - row_index * row_blocks
    )
    mine_cols = (
        lax.dynamic_slice_in_dim(slab_lists, column_index * per_column, per_column, 2)
        - column_index * column_blocks
    )
    block_ids = (mine_rows[:, :, :, None] * column_blocks + mine_cols[:, :, None, :]).reshape(-1)
    pattern_flat = block_pattern.reshape(-1)
    stored = density_matrix.reshape(row_blocks, block_size, column_blocks, block_size)
    stored = stored.transpose(0, 2, 1, 3).reshape(row_blocks * column_blocks, block_area)
    stored = stored * pattern_flat.astype(jnp.bfloat16)[:, None]
    outgoing = jnp.take(stored, block_ids, axis=0).reshape(
        row_count, column_count, per_row * per_column, block_area
    )
    flat_out = outgoing.reshape(row_count * column_count, per_row * per_column, block_area)
    incoming = lax.all_to_all(flat_out, ("row", "col"), split_axis=0, concat_axis=0, tiled=True)
    tile_matrix = incoming.reshape(
        row_count, column_count, per_row, per_column, block_size, block_size
    )
    tile_matrix = tile_matrix.transpose(0, 2, 4, 1, 3, 5).reshape(width, width)
    phi_tile = basis_values.reshape(width, -1)
    product = jnp.dot(tile_matrix, phi_tile, preferred_element_type=jnp.float32)
    rho_tile = jnp.sum(phi_tile * product, axis=0).reshape(core_density.shape)
    density = jnp.maximum(rho_tile + core_density, density_floor)
    field = potential_twice(density)
    weighted = (phi_tile * field.reshape(1, -1)).astype(jnp.bfloat16)
    local_ham = lax.dot_general(
        weighted, phi_tile, (((1,), (1,)), ((), ())), preferred_element_type=jnp.float32
    )
    returning = local_ham.reshape(
        row_count, per_row, block_size, column_count, per_column, block_size
    )
    returning = returning.transpose(0, 3, 1, 4, 2, 5).reshape(
        row_count, column_count, per_row * per_column, block_area
    )
    flat_back = returning.reshape(row_count * column_count, per_row * per_column, block_area)
    arrived = lax.all_to_all(flat_back, ("row", "col"), split_axis=0, concat_axis=0, tiled=True)
    owned = jnp.zeros((row_blocks * column_blocks, block_area), jnp.float32)
    owned = owned.at[block_ids].add(arrived.reshape(-1, block_area))
    owned = owned * pattern_flat.astype(jnp.float32)[:, None]
    dense = owned.reshape(row_blocks, column_blocks, block_size, block_size)
    dense = dense.transpose(0, 2, 1, 3).reshape(row_blocks * block_size, column_blocks * block_size)
    share = lax.psum_scatter(dense, "gz", scatter_dimension=1, tiled=True)
    terms = jnp.dot(
        share, orbitals, precision=lax.Precision.HIGHEST, preferred_element_type=jnp.float32
    )
    applied = lax.psum_scatter(terms, ("col", "gz"), scatter_dimension=0, tiled=True)
    return (share, applied)


vmem_bytes = 56 * 1024 * 1024
gathered_limit = 48 * 1024 * 1024


MESH = pl.DeviceIdType.MESH


def meet(peers):
    barrier = pltpu.get_barrier_semaphore()
    for peer in peers:
        pl.semaphore_signal(barrier, inc=1, device_id=peer, device_id_type=MESH)
    pl.semaphore_wait(barrier, len(peers))


def basis_kernel(row_count, column_count, phi, rows_out, cols_out, own_sem, send, got, got_cols):
    i, j, k = lax.axis_index("row"), lax.axis_index("col"), lax.axis_index("gz")
    across = 1 - i
    beside = lax.rem(k + 2, 4)
    twin = k + 1 - 2 * lax.rem(k, 2)
    half = column_count // row_count
    share = phi.shape[1] // half
    provider = (j // half) == i
    offset = pl.multiple_of(lax.rem(j, half) * share, share)
    x_peer, y_peer, c_peer = (across, j, k), (i, j, beside), (i, j, twin)
    up, down = lax.rem(j + 1, column_count), lax.rem(j + column_count - 1, column_count)
    z_up, z_down = (i, up, k), (i, down, k)
    meet([x_peer, y_peer, c_peer, z_up, z_down])
    has_up, has_down = j < column_count - 1, j > 0
    started, started_cols, started_twin, guarded = [], [], [], []

    def push(source, target, arrival, peer, log):
        number = len(started) + len(started_cols) + len(started_twin) + len(guarded)
        copy = pltpu.make_async_remote_copy(
            src_ref=source, dst_ref=target, send_sem=send.at[number], recv_sem=arrival,
            device_id=peer, device_id_type=MESH,
        )
        log.append(copy)
        return copy

    def arrived(out, sems, where):
        pltpu.make_async_remote_copy(
            src_ref=out.at[where], dst_ref=out.at[where], send_sem=send.at[0],
            recv_sem=sems.at[where], device_id=x_peer, device_id_type=MESH,
        ).wait_recv()

    own = (k, i, j)
    local = pltpu.make_async_copy(phi.at[i], rows_out.at[own], own_sem)
    local.start()
    push(phi.at[across], rows_out.at[own], got.at[own], x_peer, started).start()

    queue = []

    sent_z = []

    def along(source, where, peer, condition):
        copy = push(source, rows_out.at[where], got.at[where], peer, guarded)
        sent_z.append((copy, condition))
        pl.when(condition)(copy.start)

    def spread(source, where, along_y):
        if along_y:
            push(source, rows_out.at[where], got.at[where], y_peer, started).start()
        column = push(
            source.at[pl.ds(offset, share)], cols_out.at[where], got_cols.at[where], x_peer,
            started_cols,
        )
        pl.when(provider)(column.start)
        push(source, rows_out.at[where], got.at[where], c_peer, started).start()
        queue.append(where)
        if len(queue) > 3:
            relay(queue.pop(0))

    def relay(where):
        copy = push(
            cols_out.at[where], cols_out.at[where], got_cols.at[where], c_peer, started_twin
        )

        @pl.when(jnp.logical_not(provider))
        def _():
            arrived(cols_out, got_cols, where)
            copy.start()

    along(phi.at[i], own, z_up, has_up)
    along(phi.at[i], own, z_down, has_down)
    spread(phi.at[i], own, True)
    where = (k, across, j)
    arrived(rows_out, got, where)
    along(rows_out.at[where], where, z_up, has_up)
    along(rows_out.at[where], where, z_down, has_down)
    spread(rows_out.at[where], where, True)
    order = []
    for step in range(1, column_count):
        low, high = jnp.minimum(j, column_count - 1 - j), column_count - 1
        turn = (step + 1) // 2
        both = turn <= low
        sign_down = step % 2 == 1
        paired = j - turn if sign_down else j + turn
        rest = jnp.where(j < column_count - 1 - j, j + (step - low), j - (step - low))
        order.append(jnp.where(both, paired, rest))
    for other in order:
        for side in (i, across):
            where = (k, side, other)
            arrived(rows_out, got, where)
            along(rows_out.at[where], where, z_up, jnp.logical_and(other < j, has_up))
            along(rows_out.at[where], where, z_down, jnp.logical_and(other > j, has_down))
            spread(rows_out.at[where], where, True)
    slab = [(side, other) for other in order for side in (i, across)]
    for side, other in [(i, j), (across, j)] + slab:
        where = (beside, side, other)
        arrived(rows_out, got, where)
        spread(rows_out.at[where], where, False)
    while queue:
        relay(queue.pop(0))
    for depth in (twin, lax.rem(twin + 2, 4)):
        for side, other in [(i, j), (across, j)] + slab:
            arrived(rows_out, got, (depth, side, other))

    @pl.when(jnp.logical_not(provider))
    def _():
        for depth in (twin, lax.rem(twin + 2, 4)):
            for side, other in [(i, j), (across, j)] + slab:
                arrived(cols_out, got_cols, (depth, side, other))
        for copy in started_twin:
            copy.wait_send()

    @pl.when(provider)
    def _():
        for copy in started_cols:
            copy.wait_send()

    for copy in started:
        copy.wait_send()
    for copy, condition in sent_z:
        pl.when(condition)(copy.wait_send)
    local.wait()


def gather_basis(phi_tile, row_count, column_count, depth_count):
    width, cells = phi_tile.shape
    halves = phi_tile.reshape(row_count, width // row_count, cells)
    grid = (depth_count, row_count, column_count)
    count = row_count * column_count
    messages = 1 + 3 * count + 3 * 2 * count

    def body(*refs):
        basis_kernel(row_count, column_count, *refs)

    rows_phi, cols_phi = pl.pallas_call(
        body,
        in_specs=[pl.BlockSpec(memory_space=pltpu.HBM)],
        out_specs=[pl.BlockSpec(memory_space=pltpu.HBM)] * 2,
        out_shape=[
            jax.ShapeDtypeStruct(grid + (width // row_count, cells), phi_tile.dtype),
            jax.ShapeDtypeStruct(grid + (width // column_count, cells), phi_tile.dtype),
        ],
        scratch_shapes=[
            pltpu.SemaphoreType.DMA,
            pltpu.SemaphoreType.DMA((messages,)),
            pltpu.SemaphoreType.DMA(grid),
            pltpu.SemaphoreType.DMA(grid),
        ],
        compiler_params=pltpu.CompilerParams(collective_id=0, has_side_effects=True),
        name="gather_basis",
    )(halves)
    tiles = depth_count * count
    return (
        rows_phi.reshape(tiles, width // row_count, cells),
        cols_phi.reshape(tiles, width // column_count, cells),
    )


def sum_kernel(row_count, column_count, depth_count, partial, out, slots, slabs, send, got, got_slab):
    i, j, k = lax.axis_index("row"), lax.axis_index("col"), lax.axis_index("gz")
    count = row_count * column_count
    me = i * column_count + j
    peers = [lax.rem(me + step, count) for step in range(1, count)]
    depths = [lax.rem(k + step, depth_count) for step in range(1, depth_count)]
    ids = [(peer // column_count, lax.rem(peer, column_count), k) for peer in peers]
    depth_ids = [(i, j, depth) for depth in depths]
    meet(ids + depth_ids)
    copies = []
    for number, peer in enumerate(ids):
        copy = pltpu.make_async_remote_copy(
            src_ref=partial, dst_ref=slots.at[me], send_sem=send.at[number],
            recv_sem=got.at[me], device_id=peer, device_id_type=MESH,
        )
        copy.start()
        copies.append(copy)
    slots[me] = partial[...]
    for peer in peers:
        pltpu.make_async_remote_copy(
            src_ref=partial, dst_ref=slots.at[peer], send_sem=send.at[0],
            recv_sem=got.at[peer], device_id=ids[0], device_id_type=MESH,
        ).wait_recv()
    summed = slots[0]
    for number in range(1, count):
        summed = summed + slots[number]
    slabs[k] = summed
    for number, peer in enumerate(depth_ids):
        copy = pltpu.make_async_remote_copy(
            src_ref=slabs.at[k], dst_ref=slabs.at[k], send_sem=send.at[count - 1 + number],
            recv_sem=got_slab.at[k], device_id=peer, device_id_type=MESH,
        )
        copy.start()
        copies.append(copy)
    for depth in depths:
        pltpu.make_async_remote_copy(
            src_ref=partial, dst_ref=slabs.at[depth], send_sem=send.at[0],
            recv_sem=got_slab.at[depth], device_id=ids[0], device_id_type=MESH,
        ).wait_recv()
    out[...] = slabs[...]
    for copy in copies:
        copy.wait_send()


def sum_density(partial, row_count, column_count, depth_count):
    count = row_count * column_count

    def body(*refs):
        sum_kernel(row_count, column_count, depth_count, *refs)

    return pl.pallas_call(
        body,
        in_specs=[pl.BlockSpec(memory_space=pltpu.VMEM)],
        out_specs=pl.BlockSpec(memory_space=pltpu.VMEM),
        out_shape=jax.ShapeDtypeStruct((depth_count,) + partial.shape, partial.dtype),
        scratch_shapes=[
            pltpu.VMEM((count,) + partial.shape, partial.dtype),
            pltpu.VMEM((depth_count,) + partial.shape, partial.dtype),
            pltpu.SemaphoreType.DMA((count + depth_count,)),
            pltpu.SemaphoreType.DMA((count,)),
            pltpu.SemaphoreType.DMA((depth_count,)),
        ],
        compiler_params=pltpu.CompilerParams(collective_id=1, has_side_effects=True),
        name="sum_density",
    )(partial)


def applied_kernel(column_count, terms, out, c_got, y_send, y_got, z_send, z_got, send, got):
    i, j, k = lax.axis_index("row"), lax.axis_index("col"), lax.axis_index("gz")
    y, c = k // 2, lax.rem(k, 2)
    y_peer, c_peer = (i, j, lax.rem(k + 2, 4)), (i, j, k + 1 - 2 * c)
    others = [lax.rem(j + step, column_count) for step in range(1, column_count)]
    z_peers = [(i, other, k) for other in others]
    meet([y_peer, c_peer] + z_peers)

    def push(number, source, target, peer):
        copy = pltpu.make_async_remote_copy(
            src_ref=source, dst_ref=target, send_sem=send.at[number], recv_sem=got.at[number],
            device_id=peer, device_id_type=MESH,
        )
        copy.start()
        return copy

    order = others + [j]
    first, second, third, last = [], [], [], []
    for n, other in enumerate(order):
        first.append(push(n, terms.at[1 - y, 1 - c, other], c_got.at[0, other], c_peer))
    for n, other in enumerate(order):
        second.append(
            push(column_count + n, terms.at[y, 1 - c, other], c_got.at[1, other], c_peer)
        )
    for n, other in enumerate(order):
        first[n].wait_recv()
        y_send[other] = terms[1 - y, c, other] + c_got[0, other]
        third.append(push(2 * column_count + n, y_send.at[other], y_got.at[other], y_peer))
    for n, other in enumerate(order):
        second[n].wait_recv()
        third[n].wait_recv()
        z_send[other] = terms[y, c, other] + c_got[1, other] + y_got[other]
        if n < column_count - 1:
            last.append(push(3 * column_count + n, z_send.at[other], z_got.at[n], z_peers[n]))
    total = z_send[j]
    for number, copy in enumerate(last):
        copy.wait_recv()
        total = total + z_got[number]
    out[...] = total
    for copy in first + second + third + last:
        copy.wait_send()


def sum_applied(terms, column_count):
    rows, norb = terms.shape[3:]
    part = (column_count, rows, norb)

    def body(*refs):
        applied_kernel(column_count, *refs)

    return pl.pallas_call(
        body,
        in_specs=[pl.BlockSpec(memory_space=pltpu.VMEM)],
        out_specs=pl.BlockSpec(memory_space=pltpu.VMEM),
        out_shape=jax.ShapeDtypeStruct((rows, norb), terms.dtype),
        scratch_shapes=[
            pltpu.VMEM((2,) + part, terms.dtype),
            pltpu.VMEM(part, terms.dtype),
            pltpu.VMEM(part, terms.dtype),
            pltpu.VMEM(part, terms.dtype),
            pltpu.VMEM((column_count - 1, rows, norb), terms.dtype),
            pltpu.SemaphoreType.DMA((4 * column_count,)),
            pltpu.SemaphoreType.DMA((4 * column_count,)),
        ],
        compiler_params=pltpu.CompilerParams(
            collective_id=2, has_side_effects=True, vmem_limit_bytes=vmem_bytes // 2
        ),
        name="sum_applied",
    )(terms)


def density_kernel(per_row, per_column, size, counts, lists_ref, pattern_ref, place_ref, *refs):
    strips = refs[:per_row]
    phi_rows, phi_near, phi_far, out, picked, padded = refs[per_row:]
    pair_width = 2 * size
    row_blocks, column_blocks = pattern_ref.shape
    tile = pl.program_id(0) * counts[2] + place_ref[5]
    rows = [lists_ref[tile, place_ref[3] * per_row + m] for m in range(per_row)]
    rows = [row - place_ref[3] * row_blocks for row in rows]
    for n in range(per_column):
        column = lists_ref[tile, place_ref[4] * per_column + n] - place_ref[4] * column_blocks
        start = pl.multiple_of((column // 2) * pair_width, pair_width)
        odd = column % 2
        span = slice(n * size, (n + 1) * size)
        values = jnp.where(place_ref[1] == 1, phi_near[0, span, :], phi_far[0, span, :])
        for half in range(2):
            padded[n * pair_width + half * size : n * pair_width + (half + 1) * size, :] = (
                jnp.where(odd == half, values, jnp.zeros_like(values))
            )
        for m in range(per_row):
            block = strips[m][:, pl.ds(start, pair_width)]
            kept = pattern_ref[rows[m], column] != 0
            picked[m * size : (m + 1) * size, n * pair_width : (n + 1) * pair_width] = jnp.where(
                kept, block, jnp.zeros_like(block)
            )
    product = jnp.dot(picked[...], padded[...], preferred_element_type=jnp.float32)
    rho = jnp.sum(phi_rows[0].astype(jnp.float32) * product, axis=0, keepdims=True)
    out[0] = rho


def partial_density(density_matrix, rows_phi, cols_phi, lists, pattern, place, size, counts):
    tiles, cells = counts[0] * counts[1], rows_phi.shape[2]
    per_row, per_column = lists.shape[1] // counts[0], lists.shape[1] // counts[1]
    row_blocks = pattern.shape[0]
    columns = density_matrix.shape[1]

    def strip_spec(m):
        def strip(t, lists, pattern, place):
            row = lists[t * counts[2] + place[5], place[3] * per_row + m]
            return row - place[3] * row_blocks, 0

        return pl.BlockSpec((size, columns), strip)

    grid_spec = pltpu.PrefetchScalarGridSpec(
        num_scalar_prefetch=3,
        grid=(tiles,),
        in_specs=[strip_spec(m) for m in range(per_row)]
        + [
            pl.BlockSpec(
                (1, per_row * size, cells),
                lambda t, lists, pattern, place: (place[2] + t, 0, 0),
            ),
            pl.BlockSpec(
                (1, per_column * size, cells),
                lambda t, lists, pattern, place: ((place[2] + t) * place[1], place[0], 0),
            ),
            pl.BlockSpec(
                (1, per_column * size, cells),
                lambda t, lists, pattern, place: ((place[2] + t) * (1 - place[1]), 0, 0),
            ),
        ],
        out_specs=pl.BlockSpec((1, 1, cells), lambda t, lists, pattern, place: (t, 0, 0)),
        scratch_shapes=[
            pltpu.VMEM((per_row * size, 2 * per_column * size), jnp.bfloat16),
            pltpu.VMEM((2 * per_column * size, cells), jnp.bfloat16),
        ],
    )

    def body(*refs):
        density_kernel(per_row, per_column, size, counts, *refs)

    return pl.pallas_call(
        body,
        grid_spec=grid_spec,
        out_shape=jax.ShapeDtypeStruct((tiles, 1, cells), jnp.float32),
        compiler_params=pltpu.CompilerParams(vmem_limit_bytes=vmem_bytes),
        cost_estimate=pl.CostEstimate(
            flops=4 * tiles * per_row * per_column * size * size * cells,
            bytes_accessed=tiles * per_row * size * columns * 2,
            transcendentals=0,
        ),
        name="partial_density",
    )(lists, pattern, place, *([density_matrix] * per_row), rows_phi, rows_phi, cols_phi)


def hamiltonian_kernel(
    per_row, per_column, size, owned, counts, together, column_blocks, lists_ref, place_ref,
    phi_rows, phi_near, phi_far, field, keep, upper, lower, out, terms, total, weighted, padded,
    sems,
):
    step = pl.program_id(0)
    pair_width = 2 * size
    slab = counts[0] * counts[1]
    row_blocks = total.shape[0] // size

    @pl.when(step == 0)
    def _():
        total[...] = jnp.zeros_like(total)

    for inner in range(together):
        number = step * together + inner
        tile = lax.rem(number, slab) * counts[2] + number // slab
        base = place_ref[4] * column_blocks + place_ref[5] * owned
        listed = [lists_ref[tile, place_ref[4] * per_column + n] - base for n in range(per_column)]
        weighted[...] = (phi_rows[inner].astype(jnp.float32) * field[inner]).astype(jnp.bfloat16)
        for pair in range(owned // 2):
            sources = []
            for half in range(2):
                source = jnp.int32(-1)
                for n in range(per_column):
                    source = jnp.where(listed[n] == 2 * pair + half, n, source)
                sources.append(source)

            @pl.when(jnp.maximum(sources[0], sources[1]) >= 0)
            def _():
                for half, source in enumerate(sources):
                    span = pl.ds(pl.multiple_of(jnp.maximum(source, 0) * size, size), size)
                    values = jnp.where(
                        place_ref[1] == 1, phi_near[inner, span, :], phi_far[inner, span, :]
                    )
                    padded[half * size : (half + 1) * size, :] = jnp.where(
                        source >= 0, values, jnp.zeros_like(values)
                    )
                product = lax.dot_general(
                    weighted[...],
                    padded[...],
                    (((1,), (1,)), ((), ())),
                    preferred_element_type=jnp.float32,
                )
                span = slice(pair * pair_width, (pair + 1) * pair_width)
                for m in range(per_row):
                    row = lists_ref[tile, place_ref[3] * per_row + m] - place_ref[3] * row_blocks
                    start = pl.multiple_of(row * size, size)
                    total[pl.ds(start, size), span] += product[m * size : (m + 1) * size]

    @pl.when(step == pl.num_programs(0) - 1)
    def _():
        high = terms.shape[3]
        parts = high // size
        copies = []
        norb = lower.shape[1]
        for chunk in range(total.shape[0] // high):
            for part in range(parts):
                block = chunk * parts + part
                span = slice(block * size, (block + 1) * size)
                total[span, :] = total[span, :] * keep[block : block + 1, :]
            span = slice(chunk * high, (chunk + 1) * high)
            copy = pltpu.make_async_copy(total.at[span], out.at[span], sems.at[chunk])
            copy.start()
            copies.append(copy)
            values = total[span, :]
            coarse = values.astype(jnp.bfloat16)
            fine = (values - coarse.astype(jnp.float32)).astype(jnp.bfloat16)
            first = jnp.dot(coarse, upper[...], preferred_element_type=jnp.float32)
            second = jnp.dot(fine, upper[:, :norb], preferred_element_type=jnp.float32)
            depth = chunk % counts[2]
            terms[depth // 2, depth % 2, chunk // counts[2]] = (
                first[:, :norb] + (first[:, norb:] + second)
            )
        for copy in copies:
            copy.wait()


def owned_hamiltonian(rows_phi, cols_phi, field, lists, place, keep, orbitals, size, counts):
    tiles, width, cells = rows_phi.shape
    per_row, per_column = lists.shape[1] // counts[0], lists.shape[1] // counts[1]
    high = keep.shape[0] * size
    wide = keep.shape[1]
    owned = wide // size
    norb = orbitals.shape[1]
    together = 4
    chunks = counts[1] * counts[2]
    rounded = lax.reduce_precision(orbitals, exponent_bits=8, mantissa_bits=7)
    coarse = rounded.astype(jnp.bfloat16)
    fine = (orbitals - rounded).astype(jnp.bfloat16)
    upper = jnp.concatenate([coarse, fine], axis=1)
    term_shape = (2, 2, counts[1], high // chunks, norb)
    grid_spec = pltpu.PrefetchScalarGridSpec(
        num_scalar_prefetch=2,
        grid=(tiles // together,),
        in_specs=[
            pl.BlockSpec((together, per_row * size, cells), lambda t, lists, place: (t, 0, 0)),
            pl.BlockSpec(
                (together, per_column * size, cells),
                lambda t, lists, place: (t * place[1], place[0], 0),
            ),
            pl.BlockSpec(
                (together, per_column * size, cells),
                lambda t, lists, place: (t * (1 - place[1]), 0, 0),
            ),
            pl.BlockSpec((together, 1, cells), lambda t, lists, place: (t, 0, 0)),
            pl.BlockSpec(keep.shape, lambda t, lists, place: (0, 0)),
            pl.BlockSpec(upper.shape, lambda t, lists, place: (0, 0)),
            pl.BlockSpec(coarse.shape, lambda t, lists, place: (0, 0)),
        ],
        out_specs=[
            pl.BlockSpec(memory_space=pltpu.HBM),
            pl.BlockSpec(term_shape, lambda t, lists, place: (0, 0, 0, 0, 0)),
        ],
        scratch_shapes=[
            pltpu.VMEM((high, wide), jnp.float32),
            pltpu.VMEM((per_row * size, cells), jnp.bfloat16),
            pltpu.VMEM((2 * size, cells), jnp.bfloat16),
            pltpu.SemaphoreType.DMA((chunks,)),
        ],
    )

    def body(*refs):
        hamiltonian_kernel(
            per_row, per_column, size, owned, counts, together, owned * counts[2], *refs
        )

    return pl.pallas_call(
        body,
        grid_spec=grid_spec,
        out_shape=[
            jax.ShapeDtypeStruct((high, wide), jnp.float32),
            jax.ShapeDtypeStruct(term_shape, jnp.float32),
        ],
        compiler_params=pltpu.CompilerParams(vmem_limit_bytes=vmem_bytes),
        name="owned_hamiltonian",
    )(lists, place, rows_phi, rows_phi, cols_phi, field, keep, upper, coarse)


def whole_potential(density):
    def difference(values, direction):
        return (jnp.roll(values, -1, direction) - jnp.roll(values, 1, direction)) / (2.0 * spacing)

    gradients = [difference(density, direction) for direction in range(3)]
    grad_square = (
        gradients[0] * gradients[0] + gradients[1] * gradients[1] + gradients[2] * gradients[2]
    )
    first, second = jax.grad(total_energy, argnums=(0, 1))(density, grad_square)
    divergence = sum(
        difference(2.0 * second * gradients[direction], direction) for direction in range(3)
    )
    return first - divergence


def gathered(density_matrix, block_pattern, tile_lists, basis_values, core_density, orbitals):
    row_count = lax.axis_size("row")
    column_count = lax.axis_size("col")
    depth_count = lax.axis_size("gz")
    row_index = lax.axis_index("row")
    column_index = lax.axis_index("col")
    depth_index = lax.axis_index("gz")
    row_blocks, column_blocks = block_pattern.shape
    size = density_matrix.shape[0] // row_blocks
    tiles, listed = tile_lists.shape
    owned = column_blocks // depth_count
    cells = core_density.size
    phi_tile = basis_values.reshape(listed * size, cells)

    slab = row_count * column_count
    counts = (row_count, column_count, depth_count)
    half = column_count // row_count
    near = (column_index // half == row_index).astype(jnp.int32)
    place = [column_index % half, near, depth_index * slab, row_index, column_index, depth_index]
    place = jnp.stack(place).astype(jnp.int32)
    own_pattern = lax.dynamic_slice_in_dim(block_pattern, depth_index * owned, owned, 1)
    keep = jnp.repeat(own_pattern.astype(jnp.float32), size, axis=1)

    rows_phi, cols_phi = gather_basis(phi_tile, row_count, column_count, depth_count)
    partial = partial_density(
        density_matrix, rows_phi, cols_phi, tile_lists, block_pattern, place, size, counts
    )
    partial = partial.reshape(slab, cells)
    own_tile = (row_index * column_count + column_index) == jnp.arange(slab)[:, None]
    partial = partial + jnp.where(own_tile, core_density.reshape(1, cells), 0.0)
    parts = sum_density(partial, row_count, column_count, depth_count)
    tile_shape = core_density.shape
    grid = parts.reshape((depth_count, row_count, column_count) + tile_shape)
    grid = grid.transpose(1, 3, 2, 4, 0, 5).reshape(
        row_count * tile_shape[0], column_count * tile_shape[1], depth_count * tile_shape[2]
    )
    field = whole_potential(jnp.maximum(grid, density_floor))
    field = field.reshape(
        row_count, tile_shape[0], column_count, tile_shape[1], depth_count, tile_shape[2]
    )
    field = field.transpose(4, 0, 2, 1, 3, 5).reshape(tiles, 1, cells)
    hamiltonian, terms = owned_hamiltonian(
        rows_phi, cols_phi, field, tile_lists, place, keep, orbitals, size, counts
    )
    applied = sum_applied(terms, column_count)
    return hamiltonian, applied


def shards(density_matrix, block_pattern, tile_lists, basis_values, core_density, orbitals):
    arguments = (
        density_matrix, block_pattern, tile_lists, basis_values, core_density, orbitals,
    )
    counts = lax.axis_size("row"), lax.axis_size("col"), lax.axis_size("gz")
    fits = tile_lists.shape[0] * basis_values.size * 2 <= gathered_limit
    fits = fits and counts[0] == 2 and counts[1] % 2 == 0 and counts[2] == 4
    return gathered(*arguments) if fits else exchanged(*arguments)


def solution(mesh):
    placed = (
        P("row", "col"),
        P("row", "col"),
        P(),
        P("row", "col", "gz", None, None),
        P("row", "col", "gz"),
        P(("col", "gz"), None),
    )
    return jax.shard_map(
        shards,
        mesh=mesh,
        in_specs=placed,
        out_specs=(P("row", ("col", "gz")), P(("row", "col", "gz"), None)),
        check_vma=False,
    )
```
